256 devices in a mesh: member: 8 (over x, core), seq: 32 (over z, y).
Axes of the slice: x: 4, y: 4, z: 8, core: 2. Of those that a mesh axis runs over, the one named last changes fastest.
Arguments:
- vertex_embedding_matrix: bfloat16 [8, 16384, 1024], P('member', 'seq'), may hold values from -6 to 6
- norm_gain: float32 [1024], replicated, may hold values from 0.25 to 1.75
- qkv_weight: bfloat16 [1024, 3072], replicated, may hold values from -0.25 to 0.25
- out_weight: bfloat16 [1024, 1024], replicated, may hold values from -0.1875 to 0.1875
- window_reach: int32 [16384], P('seq'), may hold values from 1 to 512, as said below
- decode_weight: bfloat16 [1024, 100], replicated, may hold values from -0.1875 to 0.1875
- cell_nodes: int32 [3, 131072], P(None, 'seq'), may hold values from 0 to 16383, as said below
- cell_coeffs: float32 [3, 131072], P(None, 'seq'), may hold values from 0.2 to 0.6
- targets: bfloat16 [100, 131072], P(None, 'seq'), may hold values from -6 to 6
- area_weight: float32 [131072], P('seq'), as said below
Outputs:
- predicted_maps: bfloat16 [8, 100, 131072], P('member', None, 'seq')
- scoring_penalty: float32 [], replicated
- readout_matrix_derivative: float32 [1024, 100], replicated
The draws below stay inside these ranges and needn't reach their ends.
Inputs may be any that keep to these rules, and one draw needn't show every extreme that they name: `window_reach`: each node reaches at least one neighbour; the largest reach 512 occurs in every draw. `cell_nodes`: the nodes of cell c lie within 512 positions of c * 512 // 4096. `area_weight`: Positive.
All inputs are finite; a program needn't handle non-finite values.
Results may differ from the reference program's by a relative error of at most 0.009.
Values may be sent and summed in bfloat16 or wider, within the bound.
No kernel may reach another device: no remote copies, remote signals or barrier semaphores. Data moves between devices by JAX's collectives and lax.ppermute only.
A program may use at most 128 MiB of HBM per device.

```python
import jax
import jax.numpy as jnp
from jax import lax

D = 1024
HEADS = 16
VARS = 100
K = 3
HALF = 512
NODE_DEV = 512
CELL_DEV = 4096
MEMBERS = 8
NODES = 16384
CELLS = 131072


def draw_vertex_embedding_matrix(key, part):
    key = jax.random.fold_in(key, 5)
    noise_key = jax.random.fold_in(key, 0)
    noise = jnp.clip(jax.random.normal(noise_key, (MEMBERS, NODES, D), jnp.float32), -6.0, 6.0)
    state = noise
    return state.astype(jnp.bfloat16)


def draw_qkv_weight(key, part):
    key = jax.random.fold_in(key, 7)
    scale = D ** (-0.5)
    base = jnp.clip(jax.random.normal(key, (D, 3 * D), jnp.float32), -6.0, 6.0) * scale
    return base.astype(jnp.bfloat16)


def draw_window_reach(key, part):
    key = jax.random.fold_in(key, 11)
    reach = jax.random.randint(key, (NODES,), max(1, HALF // 4), HALF + 1)
    place = jnp.arange(NODES, dtype=jnp.int32)
    return jnp.where(place % 17 == 0, HALF, reach).astype(jnp.int32)


def draw_cell_nodes(key, part):
    key = jax.random.fold_in(key, 23)
    cells = jnp.arange(CELLS, dtype=jnp.int32)
    center = cells * NODE_DEV // CELL_DEV
    offset = jax.random.randint(key, (K, CELLS), -NODE_DEV, NODE_DEV + 1)
    return jnp.clip(center[None, :] + offset, 0, NODES - 1).astype(jnp.int32)


def draw_area_weight(key, part):
    key = jax.random.fold_in(key, 37)
    place = jnp.arange(CELLS, dtype=jnp.float32) / CELLS
    base = 1.0 + 2.0 * place
    rough = jnp.exp(jax.random.uniform(key, (CELLS,), jnp.float32, -0.693, 0.693))
    return (base * rough).astype(jnp.float32)


def block_scale(rng, extent, pieces, least, top_value):
    factor_of, own = 1.0, jax.random.fold_in(rng, 6)
    for dim, blocks in pieces:
        steps = jnp.exp(jax.random.uniform(jax.random.fold_in(own, dim), (blocks,), jnp.float32, least / len(pieces), top_value / len(pieces)))
        factor_of = factor_of * jnp.repeat(steps, extent[dim] // blocks).reshape([-1 if axis == dim else 1 for axis in range(len(extent))])
    return factor_of


def centred(rng, shape, scale, most, pieces=(), kind=jnp.bfloat16):
    gain = block_scale(rng, shape, pieces, -0.22, 0.18) if pieces else 1.0
    array = jax.random.normal(rng, shape, jnp.float32) * scale * gain
    return jnp.minimum(jnp.maximum(array, -most), most).astype(kind)


def setup_inputs(seed: int = 0) -> dict:
    key_list = jax.random.split(jax.random.key(seed), 11)
    vertex_embedding_matrix = draw_vertex_embedding_matrix(jax.random.fold_in(key_list[10], 71), 0)
    norm_gain = jnp.clip(1.0 + 0.15 * jax.random.normal(key_list[1], (D,), jnp.float32), 0.25, 1.75)
    qkv_weight = draw_qkv_weight(jax.random.fold_in(key_list[10], 71), 0)
    out_weight = centred(key_list[3], (D, D), D ** -0.5, 0.1875)
    window_reach = draw_window_reach(jax.random.fold_in(key_list[10], 71), 0)
    decode_weight = centred(key_list[5], (D, VARS), D ** -0.5, 0.1875)
    cell_nodes = draw_cell_nodes(jax.random.fold_in(key_list[10], 71), 0)
    cell_coeffs = jnp.clip(0.2 + 0.400000021 * jax.random.uniform(key_list[7], (K, CELLS), jnp.float32) ** block_scale(key_list[7], (K, CELLS), ((1, 32),), -0.2, 0.2), 0.2, 0.6)
    targets = centred(key_list[8], (VARS, CELLS), 1.0, 6.0, ((1, 32),))
    area_weight = draw_area_weight(jax.random.fold_in(key_list[10], 71), 0)
    return dict(vertex_embedding_matrix=vertex_embedding_matrix, norm_gain=norm_gain, qkv_weight=qkv_weight, out_weight=out_weight, window_reach=window_reach, decode_weight=decode_weight, cell_nodes=cell_nodes, cell_coeffs=cell_coeffs, targets=targets, area_weight=area_weight)


ALPHA = 0.95
SOFTNESS = 0.01

def soft_size(value):
    return jnp.sqrt(value * value + SOFTNESS)

def slope(value):
    return value / jnp.sqrt(value * value + SOFTNESS)

def window_attention(query, keyval, reach, start, total):
    rows = query.shape[0]
    span = keyval.shape[0]
    width = query.shape[1]
    head_dim = width // HEADS
    query_place = start + jnp.arange(rows, dtype=jnp.int32)
    key_place = start - HALF + jnp.arange(span, dtype=jnp.int32)
    inside = (key_place >= 0) & (key_place < total)
    allowed = (jnp.abs(query_place[:, None] - key_place[None, :]) <= reach[:, None]) & inside[None, :]
    query_heads = query.reshape(rows, HEADS, head_dim).astype(jnp.float32)
    key_heads = keyval[:, :width].reshape(span, HEADS, head_dim).astype(jnp.float32)
    value_heads = keyval[:, width:].reshape(span, HEADS, head_dim).astype(jnp.float32)
    scores = jnp.einsum('qhd,khd->hqk', query_heads, key_heads) * head_dim ** (-0.5)
    scores = jnp.where(allowed[None], scores, jnp.float32(-1e+30))
    row_max = lax.optimization_barrier(jnp.max(scores, axis=-1, keepdims=True))
    exponent = jnp.exp(scores - row_max)
    probs = (exponent / lax.optimization_barrier(jnp.sum(exponent, axis=-1, keepdims=True))).astype(jnp.bfloat16)
    mixed = jnp.einsum('hqk,khd->qhd', probs.astype(jnp.float32), value_heads)
    return mixed.astype(jnp.bfloat16).reshape(rows, width)

def attend(normed, qkv_weight, reach):
    qkv = jnp.dot(normed, qkv_weight, preferred_element_type=jnp.float32).astype(jnp.bfloat16)
    query = qkv[:, :D]
    padded = jnp.pad(qkv[:, D:], ((HALF, HALF), (0, 0)))
    blocks = NODES // NODE_DEV

    def one_block(index):
        start = (index * NODE_DEV).astype(jnp.int32)
        block_query = lax.dynamic_slice_in_dim(query, start, NODE_DEV, 0)
        block_keyval = lax.dynamic_slice_in_dim(padded, start, NODE_DEV + 2 * HALF, 0)
        block_reach = lax.dynamic_slice_in_dim(reach, start, NODE_DEV, 0)
        return window_attention(block_query, block_keyval, block_reach, start, NODES)
    out = lax.map(one_block, jnp.arange(blocks, dtype=jnp.int32))
    return out.reshape(NODES, D)

def reference(vertex_embedding_matrix, norm_gain, qkv_weight, out_weight, window_reach, decode_weight, cell_nodes, cell_coeffs, targets, area_weight):

    def single_realization_evaluate(state):
        state_wide = state.astype(jnp.float32)
        normed = (state_wide * lax.rsqrt(lax.optimization_barrier(jnp.mean(state_wide * state_wide, axis=-1, keepdims=True)) + 1e-05) * norm_gain).astype(jnp.bfloat16)
        attended = attend(normed, qkv_weight, window_reach)
        latent = (state_wide + jnp.dot(attended, out_weight, preferred_element_type=jnp.float32)).astype(jnp.bfloat16)
        values = jnp.dot(latent, decode_weight, preferred_element_type=jnp.float32).astype(jnp.bfloat16)
        picked = values[cell_nodes].astype(jnp.float32)
        lattice_quantities = lax.optimization_barrier(jnp.sum(cell_coeffs[:, :, None] * picked, axis=0))
        return (latent, lattice_quantities.T.astype(jnp.bfloat16))
    hidden_embedding, predicted_maps = lax.map(single_realization_evaluate, vertex_embedding_matrix)
    sample_predictions_stacked = predicted_maps.astype(jnp.float32)
    truth = targets.astype(jnp.float32)
    count = MEMBERS
    fairness = (1.0 - ALPHA) / count
    skill = lax.optimization_barrier(jnp.mean(soft_size(sample_predictions_stacked - truth[None]), axis=0))

    def pair_sum(ensemble_member):
        return lax.optimization_barrier(jnp.sum(soft_size(ensemble_member[None] - sample_predictions_stacked), axis=0))
    spread = lax.optimization_barrier(jnp.sum(lax.map(pair_sum, sample_predictions_stacked), axis=0))
    score = skill - (1.0 - fairness) / (2.0 * count * (count - 1)) * spread
    scoring_penalty = jnp.sum(area_weight[None, :] * score) / CELLS

    def member_grad(pair):
        ensemble_member, latent = pair
        slopes = lax.optimization_barrier(jnp.sum(slope(ensemble_member[None] - sample_predictions_stacked), axis=0))
        grad = (slope(ensemble_member - truth) / count - (1.0 - fairness) / (count * (count - 1)) * slopes) * area_weight[None, :] / CELLS
        terms = cell_coeffs[:, :, None] * grad.T[None, :, :]
        node_grad = jax.ops.segment_sum(terms.reshape(K * CELLS, VARS), cell_nodes.reshape(K * CELLS), num_segments=NODES)
        node_grad = node_grad.astype(jnp.bfloat16)
        return jnp.dot(latent.T, node_grad, preferred_element_type=jnp.float32)
    readout_matrix_derivative = lax.optimization_barrier(jnp.sum(lax.map(member_grad, (sample_predictions_stacked, hidden_embedding)), axis=0))
    return (predicted_maps, scoring_penalty, readout_matrix_derivative)
```

```python
import functools

import jax
import jax.numpy as jnp
from jax import lax
from jax.experimental import pallas as pl
from jax.experimental.pallas import tpu as pltpu
from jax.sharding import PartitionSpec as P

HEADS = 16
HALF = 512
ALPHA = 0.95
SOFTNESS = 0.01
MASKED = -1e30
LOG2E = 1.4426950408889634
STEPS = 4
BLOCKS = 4
F32 = jnp.float32
BF16 = jnp.bfloat16


def params(mib):
    return pltpu.CompilerParams(
        dimension_semantics=("arbitrary",), vmem_limit_bytes=mib * 1024 * 1024
    )


def rows_by_rows(left, right):
    return lax.dot_general(left, right, (((1,), (1,)), ((), ())), preferred_element_type=F32)


def matmul(left, right):
    return jnp.dot(left, right, preferred_element_type=F32)


def layer_norm(state, gain):
    wide = state.astype(F32)
    size = jnp.mean(wide * wide, axis=-1, keepdims=True)
    return (wide * lax.rsqrt(size + 1e-05) * gain).astype(BF16)


def one_head_rows(query, head):
    blank = jnp.zeros_like(query)
    return jnp.concatenate([query, blank] if head % 2 == 0 else [blank, query], axis=0)


def own_kernel(
    state_ref, gain_ref, reach_ref, wq_ref, wk_ref, wv_ref, q_ref, acc_ref, ml_ref, normed, bias
):
    nodes = state_ref.shape[0]
    half = nodes // 2

    @pl.when(pl.program_id(0) == 0)
    def _():
        normed[...] = layer_norm(state_ref[...], gain_ref[...])
        key = lax.broadcasted_iota(jnp.int32, (nodes, nodes), 0)
        place = lax.broadcasted_iota(jnp.int32, (nodes, nodes), 1)
        bias[...] = jnp.where(jnp.abs(place - key) <= reach_ref[...], 0.0, MASKED)

    width = wk_ref.shape[1]
    head_dim = 64
    rows = normed[...]
    query = (rows_by_rows(wq_ref[...], rows) * (LOG2E * head_dim**-0.5)).astype(BF16)
    q_ref[...] = query
    key = matmul(rows, wk_ref[...]).astype(BF16)
    value = rows_by_rows(wv_ref[...], rows).astype(BF16)
    for head in range(width // head_dim):
        span = slice(head * head_dim, (head + 1) * head_dim)
        pair = slice(head // 2 * 128, head // 2 * 128 + 128)
        padded_query = one_head_rows(query[span], head)
        for part in range(2):
            cols = slice(part * half, (part + 1) * half)
            scores = matmul(key[:, pair], padded_query[:, cols]) + bias[:, cols]
            top = jnp.max(scores, axis=0, keepdims=True)
            probs = jnp.exp2(scores - top)
            ml_ref[0, head : head + 1, cols] = top
            ml_ref[0, 4 + head : 5 + head, cols] = jnp.sum(probs, axis=0, keepdims=True)
            acc_ref[span, cols] = matmul(value[span], probs.astype(BF16))


def halo_kernel(
    place_ref,
    prev_ref,
    next_ref,
    state_ref,
    gain_ref,
    reach_ref,
    q_ref,
    acc_ref,
    ml_ref,
    wk_ref,
    wv_ref,
    wo_ref,
    decode_ref,
    latent_ref,
    values_ref,
    normed,
    bias,
    total,
):
    nodes = state_ref.shape[0]
    half = nodes // 2
    step = pl.program_id(0)

    @pl.when(step == 0)
    def _():
        normed[:nodes] = layer_norm(prev_ref[...], gain_ref[...])
        normed[nodes:] = layer_norm(next_ref[...], gain_ref[...])
        total[...] = jnp.zeros_like(total)
        has_prev = place_ref[0] > 0
        has_next = place_ref[0] < place_ref[1] - 1
        for part in range(2):
            key = lax.broadcasted_iota(jnp.int32, (3 * half, half), 0) + part * half
            place = lax.broadcasted_iota(jnp.int32, (3 * half, half), 1) + part * half
            before = key < nodes
            gap = jnp.where(before, place + nodes - key, key - place)
            there = (before & has_prev) | (~before & has_next)
            reach = reach_ref[:, part * half : (part + 1) * half]
            bias[part] = jnp.where((gap <= reach) & there, 0.0, MASKED)

    width = wk_ref.shape[1]
    head_dim = 64
    rows = normed[...]
    key = matmul(rows, wk_ref[...]).astype(BF16)
    value = rows_by_rows(wv_ref[...], rows).astype(BF16)
    query = q_ref[...]
    outs = []
    for head in range(width // head_dim):
        span = slice(head * head_dim, (head + 1) * head_dim)
        pair = slice(head // 2 * 128, head // 2 * 128 + 128)
        padded_query = one_head_rows(query[span], head)
        pieces = []
        for part in range(2):
            cols = slice(part * half, (part + 1) * half)
            near = slice(part * half, (part + 3) * half)
            scores = matmul(key[near, pair], padded_query[:, cols]) + bias[part]
            old_top = ml_ref[0, head : head + 1, cols]
            top = jnp.maximum(old_top, jnp.max(scores, axis=0, keepdims=True))
            probs = jnp.exp2(scores - top)
            shrink = jnp.exp2(old_top - top)
            size = ml_ref[0, 4 + head : 5 + head, cols] * shrink + jnp.sum(
                probs, axis=0, keepdims=True
            )
            mixed = acc_ref[span, cols] * shrink + matmul(value[span, near], probs.astype(BF16))
            pieces.append((mixed / size).astype(BF16))
        outs.append(jnp.concatenate(pieces, axis=1))
    attended = jnp.concatenate(outs, axis=0)
    total[...] += lax.dot_general(
        attended, wo_ref[...], (((0,), (0,)), ((), ())), preferred_element_type=F32
    )

    @pl.when(step == pl.num_programs(0) - 1)
    def _():
        latent = (state_ref[...].astype(F32) + total[...]).astype(BF16)
        latent_ref[...] = latent
        values_ref[...] = rows_by_rows(decode_ref[...], latent).astype(BF16)


def weave_kernel(index_ref, coeff_ref, out_ref):
    window, cells = out_ref.shape[1:]
    chunk = 128

    def rows(at, _):
        first = pl.multiple_of(at * chunk, chunk)
        row = lax.broadcasted_iota(jnp.int32, (chunk, cells), 0) + first
        total = jnp.zeros((chunk, cells), F32)
        for k in range(index_ref.shape[0]):
            total += jnp.where(index_ref[k : k + 1, :] == row, coeff_ref[k : k + 1, :], 0.0)
        out_ref[0, pl.ds(first, chunk), :] = total.astype(BF16)
        return 0

    lax.fori_loop(0, window // chunk, rows, 0)


def decode_kernel(prev_ref, own_ref, next_ref, weave_ref, maps_ref, send_ref, table):
    step = pl.program_id(0)
    nodes = own_ref.shape[1]

    @pl.when(step == 0)
    def _():
        table[:, :nodes] = prev_ref[...]
        table[:, nodes : 2 * nodes] = own_ref[...]
        table[:, 2 * nodes :] = next_ref[...]

    window = weave_ref.shape[1]
    first = pl.multiple_of(step * 128, 128)
    maps = matmul(table[:, pl.ds(first, window)], weave_ref[0]).astype(BF16)
    maps_ref[0] = maps
    share = send_ref.shape[2]
    for part in range(send_ref.shape[0]):
        send_ref[part] = maps[:, part * share : (part + 1) * share]


def score_kernel(members_total, cells_total, maps_ref, truth_ref, weight_ref, grad_ref, loss_ref):
    count = members_total
    fairness = (1.0 - ALPHA) / count
    own_share = 1.0 / count
    pair_share = (1.0 - fairness) / (count * (count - 1))
    rows_total, width = truth_ref.shape
    weight = weight_ref[...] / cells_total
    loss = jnp.zeros((1, width), F32)
    for first in range(0, rows_total, 16):
        rows = slice(first, min(first + 16, rows_total))
        maps = [maps_ref[m, rows, :].astype(F32) for m in range(count)]
        truth = truth_ref[rows, :].astype(F32)
        skill = None
        grads = []
        for m in range(count):
            gap = maps[m] - truth
            square = gap * gap + SOFTNESS
            inverse = lax.rsqrt(square)
            size = square * inverse
            skill = size if skill is None else skill + size
            grads.append(gap * inverse * own_share)
        spread = None
        slopes = [None] * count
        for m in range(count):
            for other in range(m + 1, count):
                gap = maps[m] - maps[other]
                square = gap * gap + SOFTNESS
                inverse = lax.rsqrt(square)
                size = square * inverse
                spread = size if spread is None else spread + size
                slope = gap * inverse
                slopes[m] = slope if slopes[m] is None else slopes[m] + slope
                slopes[other] = -slope if slopes[other] is None else slopes[other] - slope
        for m in range(count):
            grad_ref[m, rows, :] = ((grads[m] - pair_share * slopes[m]) * weight).astype(BF16)
        spread_total = 2.0 * spread + count * SOFTNESS**0.5
        score = skill * own_share - (0.5 * pair_share) * spread_total
        loss += jnp.sum(score, axis=0, keepdims=True)
    loss_ref[...] = loss * weight


def gradient_kernel(
    grad_ref, weave_ref, prev_ref, own_ref, next_ref, loss_ref, out_ref, node_grad
):
    step = pl.program_id(0)

    @pl.when(step == 0)
    def _():
        node_grad[...] = jnp.zeros_like(node_grad)

    window = weave_ref.shape[1]
    first = pl.multiple_of(step * 128, 128)
    grad = jnp.concatenate([grad_ref[part] for part in range(grad_ref.shape[0])], axis=1)
    node_grad[:, pl.ds(first, window)] += rows_by_rows(grad, weave_ref[0])

    @pl.when(step == pl.num_programs(0) - 1)
    def _():
        nodes = own_ref.shape[0]
        terms = node_grad[...].astype(BF16)
        total = matmul(terms[:, :nodes], prev_ref[...])
        total += matmul(terms[:, nodes : 2 * nodes], own_ref[...])
        total += matmul(terms[:, 2 * nodes :], next_ref[...])
        rows = total.shape[0]
        loss = jnp.sum(loss_ref[...], axis=1, keepdims=True)
        chunk = out_ref.shape[2]
        for part in range(out_ref.shape[0]):
            out_ref[part, :rows, :] = total[:, part * chunk : (part + 1) * chunk]
            out_ref[part, rows:, :] = jnp.broadcast_to(loss, (out_ref.shape[1] - rows, chunk))


def whole(*shape):
    return pl.BlockSpec(shape, lambda i: (0,) * len(shape))


def summed_over(value, axis):
    return jnp.sum(lax.all_to_all(value, axis, split_axis=0, concat_axis=0, tiled=True), axis=0)


def gathered_over(value, axis):
    copies = jnp.broadcast_to(value[None], (lax.axis_size(axis),) + value.shape)
    return lax.all_to_all(copies, axis, split_axis=0, concat_axis=0, tiled=True)


def on_device(
    vertex_embedding_matrix,
    norm_gain,
    qkv_weight,
    out_weight,
    window_reach,
    decode_weight,
    cell_nodes,
    cell_coeffs,
    targets,
    area_weight,
):
    state = vertex_embedding_matrix[0]
    nodes, width = state.shape
    variables, cells = targets.shape
    seq_count = lax.axis_size("seq")
    members = lax.axis_size("member")
    segment = lax.axis_index("seq")
    total_cells = cells * seq_count
    share = cells // members
    onward = [(i, (i + 1) % seq_count) for i in range(seq_count)]
    back = [((i + 1) % seq_count, i) for i in range(seq_count)]

    prev_state = lax.ppermute(state, "seq", onward)
    next_state = lax.ppermute(state, "seq", back)

    gain = norm_gain[None, :]
    reach = window_reach[None, :]
    query_weight = qkv_weight[:, :width].T
    value_weight = qkv_weight[:, 2 * width :].T
    group = width // STEPS
    heads = HEADS // STEPS
    query, partial, sizes = pl.pallas_call(
        own_kernel,
        grid=(STEPS,),
        in_specs=[
            whole(nodes, width),
            whole(1, width),
            whole(1, nodes),
            pl.BlockSpec((group, width), lambda i: (i, 0)),
            pl.BlockSpec((width, group), lambda i: (0, STEPS + i)),
            pl.BlockSpec((group, width), lambda i: (i, 0)),
        ],
        out_specs=[
            pl.BlockSpec((group, nodes), lambda i: (i, 0)),
            pl.BlockSpec((group, nodes), lambda i: (i, 0)),
            pl.BlockSpec((1, 2 * heads, nodes), lambda i: (i, 0, 0)),
        ],
        out_shape=[
            jax.ShapeDtypeStruct((width, nodes), BF16),
            jax.ShapeDtypeStruct((width, nodes), F32),
            jax.ShapeDtypeStruct((STEPS, 2 * heads, nodes), F32),
        ],
        scratch_shapes=[pltpu.VMEM((nodes, width), BF16), pltpu.VMEM((nodes, nodes), F32)],
        compiler_params=params(40),
        cost_estimate=pl.CostEstimate(
            flops=20 * 10**9, bytes_accessed=12 * 10**6, transcendentals=4 * 10**6
        ),
        name="own_window",
    )(state, gain, reach, query_weight, qkv_weight, value_weight)

    block = cells // BLOCKS
    block_nodes = nodes // BLOCKS
    window = 2 * nodes + block_nodes
    first = (segment - 1) * nodes + jnp.arange(cells, dtype=jnp.int32) // block * block_nodes
    weave = pl.pallas_call(
        weave_kernel,
        grid=(BLOCKS,),
        in_specs=[
            pl.BlockSpec((3, block), lambda i: (0, i)),
            pl.BlockSpec((3, block), lambda i: (0, i)),
        ],
        out_specs=pl.BlockSpec((1, window, block), lambda i: (i, 0, 0)),
        out_shape=jax.ShapeDtypeStruct((BLOCKS, window, block), BF16),
        compiler_params=params(24),
        cost_estimate=pl.CostEstimate(
            flops=10**9, bytes_accessed=10 * 10**6, transcendentals=0
        ),
        name="weave",
    )(cell_nodes - first[None, :], cell_coeffs)

    place = jnp.stack([segment, jnp.int32(seq_count)])
    latent, values = pl.pallas_call(
        halo_kernel,
        grid=(STEPS,),
        in_specs=[
            pl.BlockSpec(memory_space=pltpu.SMEM),
            whole(nodes, width),
            whole(nodes, width),
            whole(nodes, width),
            whole(1, width),
            whole(1, nodes),
            pl.BlockSpec((group, nodes), lambda i: (i, 0)),
            pl.BlockSpec((group, nodes), lambda i: (i, 0)),
            pl.BlockSpec((1, 2 * heads, nodes), lambda i: (i, 0, 0)),
            pl.BlockSpec((width, group), lambda i: (0, STEPS + i)),
            pl.BlockSpec((group, width), lambda i: (i, 0)),
            pl.BlockSpec((group, width), lambda i: (i, 0)),
            whole(variables, width),
        ],
        out_specs=[whole(nodes, width), whole(variables, nodes)],
        out_shape=[
            jax.ShapeDtypeStruct((nodes, width), BF16),
            jax.ShapeDtypeStruct((variables, nodes), BF16),
        ],
        scratch_shapes=[
            pltpu.VMEM((2 * nodes, width), BF16),
            pltpu.VMEM((2, 3 * nodes // 2, nodes // 2), F32),
            pltpu.VMEM((nodes, width), F32),
        ],
        compiler_params=params(48),
        cost_estimate=pl.CostEstimate(
            flops=30 * 10**9, bytes_accessed=16 * 10**6, transcendentals=6 * 10**6
        ),
        name="halo_window",
    )(
        place,
        prev_state,
        next_state,
        state,
        gain,
        reach,
        query,
        partial,
        sizes,
        qkv_weight,
        value_weight,
        out_weight,
        decode_weight.T,
    )

    prev_values = lax.ppermute(values, "seq", onward)
    next_values = lax.ppermute(values, "seq", back)
    later_latent, prev_values, next_values = lax.optimization_barrier(
        (latent, prev_values, next_values)
    )
    prev_latent = lax.ppermute(later_latent, "seq", onward)
    next_latent = lax.ppermute(later_latent, "seq", back)

    predicted_maps, outgoing = pl.pallas_call(
        decode_kernel,
        grid=(BLOCKS,),
        in_specs=[
            whole(variables, nodes),
            whole(variables, nodes),
            whole(variables, nodes),
            pl.BlockSpec((1, window, block), lambda i: (i, 0, 0)),
        ],
        out_specs=[
            pl.BlockSpec((1, variables, block), lambda i: (0, 0, i)),
            pl.BlockSpec((block // share, variables, share), lambda i: (i, 0, 0)),
        ],
        out_shape=[
            jax.ShapeDtypeStruct((1, variables, cells), BF16),
            jax.ShapeDtypeStruct((members, variables, share), BF16),
        ],
        scratch_shapes=[pltpu.VMEM((variables, 3 * nodes), BF16)],
        compiler_params=params(32),
        cost_estimate=pl.CostEstimate(
            flops=10**9, bytes_accessed=12 * 10**6, transcendentals=0
        ),
        name="decode_cells",
    )(prev_values, values, next_values, weave)

    incoming = lax.all_to_all(outgoing, "member", split_axis=0, concat_axis=0, tiled=True)
    member_place = lax.axis_index("member")
    truth = lax.dynamic_slice_in_dim(targets, member_place * share, share, 1)
    weight = lax.dynamic_slice_in_dim(area_weight, member_place * share, share, 0)[None, :]
    lanes = 128
    grads, loss = pl.pallas_call(
        functools.partial(score_kernel, members, total_cells),
        grid=(share // lanes,),
        in_specs=[
            pl.BlockSpec((members, variables, lanes), lambda i: (0, 0, i)),
            pl.BlockSpec((variables, lanes), lambda i: (0, i)),
            pl.BlockSpec((1, lanes), lambda i: (0, i)),
        ],
        out_specs=[
            pl.BlockSpec((members, variables, lanes), lambda i: (0, 0, i)),
            pl.BlockSpec((1, lanes), lambda i: (0, i)),
        ],
        out_shape=[
            jax.ShapeDtypeStruct((members, variables, share), BF16),
            jax.ShapeDtypeStruct((1, share), F32),
        ],
        compiler_params=params(32),
        cost_estimate=pl.CostEstimate(
            flops=10**8, bytes_accessed=2 * 10**6, transcendentals=2 * 10**6
        ),
        name="score",
    )(incoming, truth, weight)

    own_grads = lax.all_to_all(grads, "member", split_axis=0, concat_axis=0, tiled=True)
    rows = 128
    partial_grad = pl.pallas_call(
        gradient_kernel,
        grid=(BLOCKS,),
        in_specs=[
            pl.BlockSpec((block // share, variables, share), lambda i: (i, 0, 0)),
            pl.BlockSpec((1, window, block), lambda i: (i, 0, 0)),
            whole(nodes, width),
            whole(nodes, width),
            whole(nodes, width),
            whole(1, share),
        ],
        out_specs=whole(members, rows, width // members),
        out_shape=jax.ShapeDtypeStruct((members, rows, width // members), F32),
        scratch_shapes=[pltpu.VMEM((variables, 3 * nodes), F32)],
        compiler_params=params(40),
        cost_estimate=pl.CostEstimate(
            flops=2 * 10**9, bytes_accessed=14 * 10**6, transcendentals=0
        ),
        name="gradient",
    )(own_grads, weave, prev_latent, latent, next_latent, loss)

    chunk = summed_over(partial_grad, "member")
    piece = summed_over(chunk.reshape(seq_count, rows // seq_count, width // members), "seq")
    chunk = gathered_over(piece, "seq").reshape(rows, width // members)
    total = gathered_over(chunk, "member")
    scoring_penalty = total[0, variables, 0]
    readout_matrix_derivative = (
        total[:, :variables, :].transpose(0, 2, 1).reshape(width, variables)
    )
    return (predicted_maps, scoring_penalty, readout_matrix_derivative)


def solution(mesh):
    placed = (
        P("member", "seq", None),
        P(),
        P(),
        P(),
        P("seq"),
        P(),
        P(None, "seq"),
        P(None, "seq"),
        P(None, "seq"),
        P("seq"),
    )
    return jax.shard_map(
        on_device,
        mesh=mesh,
        in_specs=placed,
        out_specs=(P("member", None, "seq"), P(), P()),
        check_vma=False,
    )
```

```python
import functools

import jax
import jax.numpy as jnp
from jax import lax
from jax.experimental import pallas as pl
from jax.experimental.pallas import tpu as pltpu
from jax.sharding import PartitionSpec as P

HEADS = 16
HALF = 512
ALPHA = 0.95
SOFTNESS = 0.01
MASKED = -1e30
LOG2E = 1.4426950408889634
GROUP = 256
BLOCKS = 4
PAIR = 128
SCALE = LOG2E * 64**-0.5
BOUND = (90.0 / SCALE) ** 2
MEMBER = ("x", "core")
SEQ = ("z", "y")
F32 = jnp.float32
BF16 = jnp.bfloat16


def params(mib):
    return pltpu.CompilerParams(vmem_limit_bytes=mib * 1024 * 1024)


def rows_by_rows(left, right):
    return lax.dot_general(left, right, (((1,), (1,)), ((), ())), preferred_element_type=F32)


def matmul(left, right):
    return jnp.dot(left, right, preferred_element_type=F32)


def layer_norm(state, gain):
    wide = state.astype(F32)
    size = jnp.mean(wide * wide, axis=-1, keepdims=True)
    return (wide * lax.rsqrt(size + 1e-05) * gain).astype(BF16)


def split_heads(rows):
    lane = lax.broadcasted_iota(jnp.int32, (rows.shape[0], PAIR), 1)
    first = lane < PAIR // 2
    blank = jnp.zeros((rows.shape[0], PAIR), rows.dtype)
    heads = []
    for at in range(0, rows.shape[1], PAIR):
        pair = rows[:, at : at + PAIR]
        heads.append(jnp.where(first, pair, blank))
        heads.append(jnp.where(first, blank, pair))
    return heads


def head_norms(rows):
    lane, column = grid_of((rows.shape[1], PAIR))
    pick = jnp.where(lane // 64 == column, 1.0, 0.0).astype(BF16)
    wide = rows.astype(F32)
    sizes = matmul((wide * wide).astype(BF16), pick)
    return jnp.max(sizes.reshape(rows.shape[0] // 8, 8, PAIR), axis=0).max(axis=0, keepdims=True)


def side_by_side(left, right):
    lane = lax.broadcasted_iota(jnp.int32, left.shape, 1)
    return jnp.where(lane < PAIR // 2, left, right)


def attend_pair(queries, key, value, mask):
    mixed = []
    for query in queries:
        probs = jnp.exp2(rows_by_rows(query, key) * SCALE).astype(BF16) * mask
        mixed.append(matmul(probs, value))
    return (
        side_by_side(mixed[0][:, :PAIR], mixed[1][:, :PAIR]),
        side_by_side(mixed[0][:, PAIR:], mixed[1][:, PAIR:]),
    )


def halves(nodes):
    return [slice(0, nodes // 2), slice(nodes // 2, nodes)]


def grid_of(shape):
    return [lax.broadcasted_iota(jnp.int32, shape, dim) for dim in range(2)]


def flag(value):
    return jnp.where(value, 1.0, 0.0)


def own_kernel(
    state_ref,
    gain_ref,
    reach_ref,
    weight_ref,
    query_ref,
    acc_ref,
    size_ref,
    norm_ref,
    bound_ref,
    normed,
    mask,
    values,
):
    nodes, width = state_ref.shape
    normed[...] = layer_norm(state_ref[...], gain_ref[...])
    place, spot = grid_of((nodes, nodes))
    mask[...] = flag(jnp.abs(place - spot) <= reach_ref[...]).astype(BF16)
    values[...] = jnp.ones_like(values)
    bound = jnp.zeros((1, PAIR), F32)
    for step, first in enumerate(range(0, width, GROUP)):
        rows = normed[...]
        query = matmul(rows, weight_ref[:, first : first + GROUP]).astype(BF16)
        query_ref[:, first : first + GROUP] = query
        at = width + first
        key = matmul(rows, weight_ref[:, at : at + GROUP]).astype(BF16)
        at = 2 * width + first
        value = matmul(rows, weight_ref[:, at : at + GROUP]).astype(BF16)
        heads = split_heads(query)
        norm = head_norms(query)
        norm_ref[step : step + 1, :] = norm
        bound = jnp.maximum(bound, norm * head_norms(key))
        for pair in range(GROUP // PAIR):
            lanes = slice(pair * PAIR, (pair + 1) * PAIR)
            out = slice(first + pair * PAIR, first + (pair + 1) * PAIR)
            held = first // PAIR + pair
            values[held, :, :PAIR] = value[:, lanes]
            for part in halves(nodes):
                queries = [head[part] for head in heads[2 * pair : 2 * pair + 2]]
                acc_ref[part, out], size_ref[part, out] = attend_pair(
                    queries, key[:, lanes], values[held], mask[part, :]
                )
    bound_ref[...] = bound


def halo_kernel(
    place_ref,
    prev_ref,
    next_ref,
    state_ref,
    gain_ref,
    reach_ref,
    query_ref,
    acc_ref,
    size_ref,
    norm_ref,
    bound_ref,
    weight_ref,
    out_weight_ref,
    decode_ref,
    latent_ref,
    values_ref,
    normed,
    mask,
    values,
    attended,
):
    nodes, width = state_ref.shape
    half = nodes // 2
    has_prev = place_ref[0] > 0
    has_next = place_ref[0] < place_ref[1] - 1
    normed[:nodes] = layer_norm(prev_ref[...], gain_ref[...])
    normed[nodes:] = layer_norm(next_ref[...], gain_ref[...])
    values[...] = jnp.ones_like(values)
    for part, here in enumerate(halves(nodes)):
        place, key = [axis + part * half for axis in grid_of((half, 3 * half))]
        before = key < nodes
        gap = jnp.where(before, place + nodes - key, key - place)
        there = (before & has_prev) | (~before & has_next)
        mask[part] = flag((gap <= reach_ref[here, :]) & there).astype(BF16)

    bound = bound_ref[...]
    for step, first in enumerate(range(0, width, GROUP)):
        rows = normed[...]
        at = width + first
        key = matmul(rows, weight_ref[:, at : at + GROUP]).astype(BF16)
        at = 2 * width + first
        value = matmul(rows, weight_ref[:, at : at + GROUP]).astype(BF16)
        heads = split_heads(query_ref[:, first : first + GROUP])
        bound = jnp.maximum(bound, norm_ref[step : step + 1, :] * head_norms(key))
        for pair in range(GROUP // PAIR):
            lanes = slice(pair * PAIR, (pair + 1) * PAIR)
            out = slice(first + pair * PAIR, first + (pair + 1) * PAIR)
            held = first // PAIR + pair
            values[held, :, :PAIR] = value[:, lanes]
            for part, here in enumerate(halves(nodes)):
                near = slice(part * half, (part + 3) * half)
                queries = [head[here] for head in heads[2 * pair : 2 * pair + 2]]
                acc, size = attend_pair(queries, key[near, lanes], values[held, near], mask[part])
                acc += acc_ref[here, out]
                size += size_ref[here, out]
                attended[here, out] = (acc / size).astype(BF16)

    @pl.when(jnp.logical_not(jnp.max(bound) <= BOUND))
    def _():
        def one_pair(pair, _):
            first = pl.multiple_of(pair * PAIR, PAIR)
            out = pl.ds(first, PAIR)
            keys_at, values_at = pl.ds(width + first, PAIR), pl.ds(2 * width + first, PAIR)
            key = matmul(normed[...], weight_ref[:, keys_at]).astype(BF16)
            value = matmul(normed[...], weight_ref[:, values_at]).astype(BF16)
            own_rows = layer_norm(state_ref[...], gain_ref[...])
            own_key = matmul(own_rows, weight_ref[:, keys_at]).astype(BF16)
            own_value = matmul(own_rows, weight_ref[:, values_at]).astype(BF16)
            own_place, own_spot = grid_of((nodes, nodes))
            allowed = jnp.abs(own_place - own_spot) <= reach_ref[...]
            heads = split_heads(query_ref[:, out])
            for part, here in enumerate(halves(nodes)):
                near = slice(part * half, (part + 3) * half)
                both = []
                for head in heads:
                    far = rows_by_rows(head[here], key[near]) * SCALE
                    far = jnp.where(mask[part] > 0, far, MASKED)
                    own = rows_by_rows(head[here], own_key) * SCALE
                    own = jnp.where(allowed[here], own, MASKED)
                    top = jnp.maximum(
                        jnp.max(far, axis=1, keepdims=True), jnp.max(own, axis=1, keepdims=True)
                    )
                    far, own = jnp.exp2(far - top), jnp.exp2(own - top)
                    size = jnp.sum(far, axis=1, keepdims=True)
                    size += jnp.sum(own, axis=1, keepdims=True)
                    mixed = matmul(far.astype(BF16), value[near])
                    mixed += matmul(own.astype(BF16), own_value)
                    both.append(mixed / size)
                attended[here, out] = side_by_side(*both).astype(BF16)
            return 0

        lax.fori_loop(0, width // PAIR, one_pair, 0)

    total = state_ref[...].astype(F32) + matmul(attended[...], out_weight_ref[...])
    latent = total.astype(BF16)
    latent_ref[...] = latent
    values_ref[...] = rows_by_rows(decode_ref[...], latent).astype(BF16)


def weave_kernel(index_ref, coeff_ref, out_ref):
    blocks, window, cells = out_ref.shape
    chunk = 64
    for block in range(blocks):
        here = slice(block * cells, (block + 1) * cells)

        def rows(at, _):
            first = pl.multiple_of(at * chunk, chunk)
            row = lax.broadcasted_iota(jnp.int32, (chunk, cells), 0) + first
            total = jnp.zeros((chunk, cells), F32)
            for k in range(index_ref.shape[0]):
                total += jnp.where(index_ref[k : k + 1, here] == row, coeff_ref[k : k + 1, here], 0.0)
            out_ref[block, pl.ds(first, chunk), :] = total.astype(BF16)
            return 0

        lax.fori_loop(0, window // chunk, rows, 0)


def decode_kernel(prev_ref, own_ref, next_ref, weave_ref, maps_ref, send_ref):
    table = jnp.concatenate([prev_ref[...], own_ref[...], next_ref[...]], axis=1)
    blocks, window, cells = weave_ref.shape
    step = own_ref.shape[1] // blocks
    share = send_ref.shape[2]
    for block in range(blocks):
        maps = matmul(table[:, block * step : block * step + window], weave_ref[block]).astype(BF16)
        maps_ref[0, :, block * cells : (block + 1) * cells] = maps
        for part in range(cells // share):
            send_ref[block * (cells // share) + part] = maps[:, part * share : (part + 1) * share]


def score_kernel(members_total, cells_total, maps_ref, truth_ref, weight_ref, grad_ref, loss_ref):
    count = members_total
    fairness = (1.0 - ALPHA) / count
    own_share = 1.0 / count
    pair_share = (1.0 - fairness) / (count * (count - 1))
    rows_total, width = truth_ref.shape
    weight = weight_ref[...] / cells_total
    loss = jnp.zeros((1, width), F32)
    for first in range(0, rows_total, 16):
        rows = slice(first, min(first + 16, rows_total))
        maps = [maps_ref[m, rows, :].astype(F32) for m in range(count)]
        truth = truth_ref[rows, :].astype(F32)
        skill = None
        grads = []
        for m in range(count):
            gap = maps[m] - truth
            square = gap * gap + SOFTNESS
            inverse = lax.rsqrt(square)
            size = square * inverse
            skill = size if skill is None else skill + size
            grads.append(gap * inverse * own_share)
        spread = None
        slopes = [None] * count
        for m in range(count):
            for other in range(m + 1, count):
                gap = maps[m] - maps[other]
                square = gap * gap + SOFTNESS
                inverse = lax.rsqrt(square)
                size = square * inverse
                spread = size if spread is None else spread + size
                slope = gap * inverse
                slopes[m] = slope if slopes[m] is None else slopes[m] + slope
                slopes[other] = -slope if slopes[other] is None else slopes[other] - slope
        for m in range(count):
            grad_ref[m, rows, :] = ((grads[m] - pair_share * slopes[m]) * weight).astype(BF16)
        spread_total = 2.0 * spread + count * SOFTNESS**0.5
        score = skill * own_share - (0.5 * pair_share) * spread_total
        loss += jnp.sum(score, axis=0, keepdims=True)
    loss_ref[...] = loss * weight


def gradient_kernel(
    grad_ref,
    loss_ref,
    weave_hbm,
    prev_hbm,
    own_hbm,
    next_hbm,
    out_ref,
    node_grad,
    weave_ref,
    latent_ref,
    arrived,
):
    blocks, window, cells = weave_ref.shape
    copies = [
        pltpu.make_async_copy(weave_hbm.at[block], weave_ref.at[block], arrived.at[block])
        for block in range(blocks)
    ]
    copies += [
        pltpu.make_async_copy(source, latent_ref.at[at], arrived.at[blocks + at])
        for at, source in enumerate((prev_hbm, own_hbm, next_hbm))
    ]
    for copy in copies:
        copy.start()
    nodes = latent_ref.shape[1]
    step = nodes // blocks
    share = grad_ref.shape[2]
    node_grad[...] = jnp.zeros_like(node_grad)
    for block in range(blocks):
        parts = range(block * cells // share, (block + 1) * cells // share)
        grad = jnp.concatenate([grad_ref[part] for part in parts], axis=1)
        copies[block].wait()
        node_grad[:, block * step : block * step + window] += rows_by_rows(grad, weave_ref[block])
    terms = node_grad[...].astype(BF16)
    total = jnp.zeros((terms.shape[0], latent_ref.shape[2]), F32)
    for at in range(3):
        copies[blocks + at].wait()
        total += matmul(terms[:, at * nodes : (at + 1) * nodes], latent_ref[at])
    rows = total.shape[0]
    loss = jnp.sum(loss_ref[...], axis=1, keepdims=True)
    coarse = loss.astype(BF16).astype(F32)
    pieces, _, lanes = out_ref.shape
    splits = pieces * lanes // total.shape[1]
    each = rows // splits
    spare = out_ref.shape[1] - each
    row = lax.broadcasted_iota(jnp.int32, (spare, lanes), 0)
    tail = jnp.where(row == 0, coarse, jnp.where(row == 1, loss - coarse, 0.0)).astype(BF16)
    for piece in range(pieces):
        first = piece % splits * each
        at = piece // splits * lanes
        part = total[first : first + each, at : at + lanes].astype(BF16)
        out_ref[piece] = jnp.concatenate([part, tail], axis=0)


def summed_over(value, axes):
    parts = lax.all_to_all(value, axes, split_axis=0, concat_axis=0, tiled=True)
    return jnp.sum(parts.astype(F32), axis=0)


def gathered_over(value, axes):
    copies = jnp.broadcast_to(value[None], (lax.axis_size(axes),) + value.shape)
    return lax.all_to_all(copies, axes, split_axis=0, concat_axis=0, tiled=True)


def on_device(
    vertex_embedding_matrix,
    norm_gain,
    qkv_weight,
    out_weight,
    window_reach,
    decode_weight,
    cell_nodes,
    cell_coeffs,
    targets,
    area_weight,
):
    state = vertex_embedding_matrix[0]
    nodes, width = state.shape
    variables, cells = targets.shape
    seq_count = lax.axis_size(SEQ)
    members = lax.axis_size(MEMBER)
    segment = lax.axis_index(SEQ)
    total_cells = cells * seq_count
    share = cells // members
    onward = [(i, (i + 1) % seq_count) for i in range(seq_count)]
    back = [((i + 1) % seq_count, i) for i in range(seq_count)]

    prev_state = lax.ppermute(state, SEQ, onward)
    next_state = lax.ppermute(state, SEQ, back)

    gain = norm_gain[None, :]
    reach = window_reach[:, None]
    smem = pl.BlockSpec(memory_space=pltpu.SMEM)
    anywhere = pl.BlockSpec(memory_space=pl.ANY)
    vmem = pl.BlockSpec(memory_space=pltpu.VMEM)
    sum_type = jax.ShapeDtypeStruct((nodes, width), F32)
    query, own_acc, own_size, norms, bound = pl.pallas_call(
        own_kernel,
        in_specs=[vmem] * 4,
        out_specs=[vmem] * 5,
        out_shape=[
            jax.ShapeDtypeStruct((nodes, width), BF16),
            sum_type,
            sum_type,
            jax.ShapeDtypeStruct((width // GROUP, PAIR), F32),
            jax.ShapeDtypeStruct((1, PAIR), F32),
        ],
        scratch_shapes=[
            pltpu.VMEM((nodes, width), BF16),
            pltpu.VMEM((nodes, nodes), BF16),
            pltpu.VMEM((width // PAIR, nodes, 2 * PAIR), BF16),
        ],
        compiler_params=params(16),
        cost_estimate=pl.CostEstimate(
            flops=12 * 10**9, bytes_accessed=12 * 10**6, transcendentals=4 * 10**6
        ),
        name="own_window",
    )(state, gain, reach, qkv_weight)

    blocks = BLOCKS
    block = cells // blocks
    block_nodes = nodes // blocks
    window = 2 * nodes + block_nodes
    first = (segment - 1) * nodes + jnp.arange(cells, dtype=jnp.int32) // block * block_nodes
    weave = pl.pallas_call(
        weave_kernel,
        in_specs=[vmem, vmem],
        out_specs=vmem,
        out_shape=jax.ShapeDtypeStruct((blocks, window, block), BF16),
        compiler_params=params(4),
        cost_estimate=pl.CostEstimate(flops=10**9, bytes_accessed=10 * 10**6, transcendentals=0),
        name="weave",
    )(cell_nodes - first[None, :], cell_coeffs)
    query, weave = lax.optimization_barrier((query, weave))

    place = jnp.stack([segment, jnp.int32(seq_count)])
    latent, values = pl.pallas_call(
        halo_kernel,
        in_specs=[smem] + [vmem] * 13,
        out_specs=[vmem, vmem],
        out_shape=[
            jax.ShapeDtypeStruct((nodes, width), BF16),
            jax.ShapeDtypeStruct((variables, nodes), BF16),
        ],
        scratch_shapes=[
            pltpu.VMEM((2 * nodes, width), BF16),
            pltpu.VMEM((2, nodes // 2, 3 * nodes // 2), BF16),
            pltpu.VMEM((width // PAIR, 2 * nodes, 2 * PAIR), BF16),
            pltpu.VMEM((nodes, width), BF16),
        ],
        compiler_params=params(24),
        cost_estimate=pl.CostEstimate(
            flops=20 * 10**9, bytes_accessed=16 * 10**6, transcendentals=6 * 10**6
        ),
        name="halo_window",
    )(
        place,
        prev_state,
        next_state,
        state,
        gain,
        reach,
        query,
        own_acc,
        own_size,
        norms,
        bound,
        qkv_weight,
        out_weight,
        decode_weight.T,
    )

    prev_values = lax.ppermute(values, SEQ, onward)
    next_values = lax.ppermute(values, SEQ, back)
    later_latent, prev_values, next_values = lax.optimization_barrier(
        (latent, prev_values, next_values)
    )
    prev_latent = lax.ppermute(later_latent, SEQ, onward)
    next_latent = lax.ppermute(later_latent, SEQ, back)

    predicted_maps, outgoing = pl.pallas_call(
        decode_kernel,
        in_specs=[vmem] * 4,
        out_specs=[vmem, vmem],
        out_shape=[
            jax.ShapeDtypeStruct((1, variables, cells), BF16),
            jax.ShapeDtypeStruct((members, variables, share), BF16),
        ],
        compiler_params=params(16),
        cost_estimate=pl.CostEstimate(
            flops=10**9, bytes_accessed=12 * 10**6, transcendentals=0
        ),
        name="decode_cells",
    )(prev_values, values, next_values, weave)

    incoming = lax.all_to_all(outgoing, MEMBER, split_axis=0, concat_axis=0, tiled=True)
    member_place = lax.axis_index(MEMBER)
    truth = lax.dynamic_slice_in_dim(targets, member_place * share, share, 1)
    weight = lax.dynamic_slice_in_dim(area_weight, member_place * share, share, 0)[None, :]
    lanes = 128
    grads, loss = pl.pallas_call(
        functools.partial(score_kernel, members, total_cells),
        grid=(share // lanes,),
        in_specs=[
            pl.BlockSpec((members, variables, lanes), lambda i: (0, 0, i)),
            pl.BlockSpec((variables, lanes), lambda i: (0, i)),
            pl.BlockSpec((1, lanes), lambda i: (0, i)),
        ],
        out_specs=[
            pl.BlockSpec((members, variables, lanes), lambda i: (0, 0, i)),
            pl.BlockSpec((1, lanes), lambda i: (0, i)),
        ],
        out_shape=[
            jax.ShapeDtypeStruct((members, variables, share), BF16),
            jax.ShapeDtypeStruct((1, share), F32),
        ],
        compiler_params=params(16),
        cost_estimate=pl.CostEstimate(
            flops=10**8, bytes_accessed=2 * 10**6, transcendentals=2 * 10**6
        ),
        name="score",
    )(incoming, truth, weight)

    own_grads = lax.all_to_all(grads, MEMBER, split_axis=0, concat_axis=0, tiled=True)
    lines = lax.axis_size("y")
    pieces = members * lines
    lanes = width // members
    each = variables // lines
    rows = -(-(each + 2) // 16) * 16
    partial_grad = pl.pallas_call(
        gradient_kernel,
        in_specs=[vmem, vmem] + [anywhere] * 4,
        out_specs=vmem,
        out_shape=jax.ShapeDtypeStruct((pieces, rows, lanes), BF16),
        scratch_shapes=[
            pltpu.VMEM((variables, 3 * nodes), F32),
            pltpu.VMEM((blocks, window, block), BF16),
            pltpu.VMEM((3, nodes, width), BF16),
            pltpu.SemaphoreType.DMA((blocks + 3,)),
        ],
        compiler_params=params(58),
        cost_estimate=pl.CostEstimate(
            flops=2 * 10**9, bytes_accessed=14 * 10**6, transcendentals=0
        ),
        name="gradient",
    )(own_grads, loss, weave, prev_latent, latent, next_latent)

    piece = summed_over(partial_grad, MEMBER + ("y",))
    piece = jnp.sum(gathered_over(piece, "z"), axis=0)
    loss = piece[each : each + 1] + piece[each + 1 : each + 2]
    coarse = lax.reduce_precision(loss, 8, 7)
    piece = jnp.concatenate([piece[:each], coarse, loss - coarse], axis=0)
    piece = jnp.pad(piece, ((0, rows - each - 2), (0, 0))).astype(BF16)
    total = gathered_over(piece, MEMBER + ("y",)).astype(F32)
    scoring_penalty = total[0, each, 0] + total[0, each + 1, 0]
    readout_matrix_derivative = (
        total.reshape(members, lines, rows, lanes)[:, :, :each]
        .transpose(0, 3, 1, 2)
        .reshape(width, variables)
    )
    return (predicted_maps, scoring_penalty, readout_matrix_derivative)


def solution(mesh):
    by_links = jax.sharding.Mesh(mesh.devices.reshape(4, 2, 8, 4), MEMBER + SEQ)
    placed = (
        P(MEMBER, SEQ, None),
        P(),
        P(),
        P(),
        P(SEQ),
        P(),
        P(None, SEQ),
        P(None, SEQ),
        P(None, SEQ),
        P(SEQ),
    )
    return jax.shard_map(
        on_device,
        mesh=by_links,
        in_specs=placed,
        out_specs=(P(MEMBER, None, SEQ), P(), P()),
        check_vma=False,
    )
```

```python
import functools

import jax
import jax.numpy as jnp
from jax import lax
from jax.experimental import pallas as pl
from jax.experimental.pallas import tpu as pltpu
from jax.sharding import PartitionSpec as P

HEADS = 16
HALF = 512
ALPHA = 0.95
SOFTNESS = 0.01
MASKED = -1e30
LOG2E = 1.4426950408889634
GROUP = 256
BLOCKS = 4
PAIR = 128
SCALE = LOG2E * 64**-0.5
BOUND = (90.0 / SCALE) ** 2
MEMBER = ("x", "core")
SEQ = ("z", "y")
F32 = jnp.float32
BF16 = jnp.bfloat16


def params(mib):
    return pltpu.CompilerParams(vmem_limit_bytes=mib * 1024 * 1024)


def rows_by_rows(left, right):
    return lax.dot_general(left, right, (((1,), (1,)), ((), ())), preferred_element_type=F32)


def matmul(left, right):
    return jnp.dot(left, right, preferred_element_type=F32)


def layer_norm(state, gain):
    wide = state.astype(F32)
    size = jnp.mean(wide * wide, axis=-1, keepdims=True)
    return (wide * lax.rsqrt(size + 1e-05) * gain).astype(BF16)


def split_heads(rows):
    lane = lax.broadcasted_iota(jnp.int32, (rows.shape[0], PAIR), 1)
    first = lane < PAIR // 2
    blank = jnp.zeros((rows.shape[0], PAIR), rows.dtype)
    heads = []
    for at in range(0, rows.shape[1], PAIR):
        pair = rows[:, at : at + PAIR]
        heads.append(jnp.where(first, pair, blank))
        heads.append(jnp.where(first, blank, pair))
    return heads


def head_norms(rows):
    lane, column = grid_of((rows.shape[1], PAIR))
    pick = jnp.where(lane // 64 == column, 1.0, 0.0).astype(BF16)
    wide = rows.astype(F32)
    sizes = matmul((wide * wide).astype(BF16), pick)
    return jnp.max(sizes.reshape(rows.shape[0] // 8, 8, PAIR), axis=0).max(axis=0, keepdims=True)


def side_by_side(left, right):
    lane = lax.broadcasted_iota(jnp.int32, left.shape, 1)
    return jnp.where(lane < PAIR // 2, left, right)


def attend_pair(queries, key, value, mask):
    mixed = []
    for query in queries:
        probs = jnp.exp2(rows_by_rows(query, key) * SCALE).astype(BF16) * mask
        mixed.append(matmul(probs, value))
    return (
        side_by_side(mixed[0][:, :PAIR], mixed[1][:, :PAIR]),
        side_by_side(mixed[0][:, PAIR:], mixed[1][:, PAIR:]),
    )


def halves(nodes):
    return [slice(0, nodes // 2), slice(nodes // 2, nodes)]


def grid_of(shape):
    return [lax.broadcasted_iota(jnp.int32, shape, dim) for dim in range(2)]


def flag(value):
    return jnp.where(value, 1.0, 0.0)


def own_kernel(
    state_ref,
    gain_ref,
    reach_ref,
    weight_ref,
    query_ref,
    acc_ref,
    size_ref,
    norm_ref,
    bound_ref,
    normed,
    mask,
    values,
):
    nodes, width = state_ref.shape
    normed[...] = layer_norm(state_ref[...], gain_ref[...])
    place, spot = grid_of((nodes, nodes))
    mask[...] = flag(jnp.abs(place - spot) <= reach_ref[...]).astype(BF16)
    values[...] = jnp.ones_like(values)
    bound = jnp.zeros((1, PAIR), F32)
    for step, first in enumerate(range(0, width, GROUP)):
        rows = normed[...]
        query = matmul(rows, weight_ref[:, first : first + GROUP]).astype(BF16)
        query_ref[:, first : first + GROUP] = query
        at = width + first
        key = matmul(rows, weight_ref[:, at : at + GROUP]).astype(BF16)
        at = 2 * width + first
        value = matmul(rows, weight_ref[:, at : at + GROUP]).astype(BF16)
        heads = split_heads(query)
        norm = head_norms(query)
        norm_ref[step : step + 1, :] = norm
        bound = jnp.maximum(bound, norm * head_norms(key))
        for pair in range(GROUP // PAIR):
            lanes = slice(pair * PAIR, (pair + 1) * PAIR)
            out = slice(first + pair * PAIR, first + (pair + 1) * PAIR)
            held = first // PAIR + pair
            values[held, :, :PAIR] = value[:, lanes]
            for part in halves(nodes):
                queries = [head[part] for head in heads[2 * pair : 2 * pair + 2]]
                acc_ref[part, out], size_ref[part, out] = attend_pair(
                    queries, key[:, lanes], values[held], mask[part, :]
                )
    bound_ref[...] = bound


def halo_kernel(
    place_ref,
    prev_ref,
    next_ref,
    state_ref,
    gain_ref,
    reach_ref,
    query_ref,
    acc_ref,
    size_ref,
    norm_ref,
    bound_ref,
    weight_ref,
    out_weight_ref,
    decode_ref,
    latent_ref,
    values_ref,
    normed,
    mask,
    values,
    attended,
):
    nodes, width = state_ref.shape
    half = nodes // 2
    has_prev = place_ref[0] > 0
    has_next = place_ref[0] < place_ref[1] - 1
    normed[:nodes] = layer_norm(prev_ref[...], gain_ref[...])
    normed[nodes:] = layer_norm(next_ref[...], gain_ref[...])
    values[...] = jnp.ones_like(values)
    for part, here in enumerate(halves(nodes)):
        place, key = [axis + part * half for axis in grid_of((half, 3 * half))]
        before = key < nodes
        gap = jnp.where(before, place + nodes - key, key - place)
        there = (before & has_prev) | (~before & has_next)
        mask[part] = flag((gap <= reach_ref[here, :]) & there).astype(BF16)

    bound = bound_ref[...]
    for step, first in enumerate(range(0, width, GROUP)):
        rows = normed[...]
        at = width + first
        key = matmul(rows, weight_ref[:, at : at + GROUP]).astype(BF16)
        at = 2 * width + first
        value = matmul(rows, weight_ref[:, at : at + GROUP]).astype(BF16)
        heads = split_heads(query_ref[:, first : first + GROUP])
        bound = jnp.maximum(bound, norm_ref[step : step + 1, :] * head_norms(key))
        for pair in range(GROUP // PAIR):
            lanes = slice(pair * PAIR, (pair + 1) * PAIR)
            out = slice(first + pair * PAIR, first + (pair + 1) * PAIR)
            held = first // PAIR + pair
            values[held, :, :PAIR] = value[:, lanes]
            for part, here in enumerate(halves(nodes)):
                near = slice(part * half, (part + 3) * half)
                queries = [head[here] for head in heads[2 * pair : 2 * pair + 2]]
                acc, size = attend_pair(queries, key[near, lanes], values[held, near], mask[part])
                acc += acc_ref[here, out]
                size += size_ref[here, out]
                attended[here, out] = (acc / size).astype(BF16)

    @pl.when(jnp.logical_not(jnp.max(bound) <= BOUND))
    def _():
        def one_pair(pair, _):
            first = pl.multiple_of(pair * PAIR, PAIR)
            out = pl.ds(first, PAIR)
            keys_at, values_at = pl.ds(width + first, PAIR), pl.ds(2 * width + first, PAIR)
            key = matmul(normed[...], weight_ref[:, keys_at]).astype(BF16)
            value = matmul(normed[...], weight_ref[:, values_at]).astype(BF16)
            own_rows = layer_norm(state_ref[...], gain_ref[...])
            own_key = matmul(own_rows, weight_ref[:, keys_at]).astype(BF16)
            own_value = matmul(own_rows, weight_ref[:, values_at]).astype(BF16)
            own_place, own_spot = grid_of((nodes, nodes))
            allowed = jnp.abs(own_place - own_spot) <= reach_ref[...]
            heads = split_heads(query_ref[:, out])
            for part, here in enumerate(halves(nodes)):
                near = slice(part * half, (part + 3) * half)
                both = []
                for head in heads:
                    far = rows_by_rows(head[here], key[near]) * SCALE
                    far = jnp.where(mask[part] > 0, far, MASKED)
                    own = rows_by_rows(head[here], own_key) * SCALE
                    own = jnp.where(allowed[here], own, MASKED)
                    top = jnp.maximum(
                        jnp.max(far, axis=1, keepdims=True), jnp.max(own, axis=1, keepdims=True)
                    )
                    far, own = jnp.exp2(far - top), jnp.exp2(own - top)
                    size = jnp.sum(far, axis=1, keepdims=True)
                    size += jnp.sum(own, axis=1, keepdims=True)
                    mixed = matmul(far.astype(BF16), value[near])
                    mixed += matmul(own.astype(BF16), own_value)
                    both.append(mixed / size)
                attended[here, out] = side_by_side(*both).astype(BF16)
            return 0

        lax.fori_loop(0, width // PAIR, one_pair, 0)

    total = state_ref[...].astype(F32) + matmul(attended[...], out_weight_ref[...])
    latent = total.astype(BF16)
    latent_ref[...] = latent
    values_ref[...] = rows_by_rows(decode_ref[...], latent).astype(BF16)


def weave_kernel(index_ref, coeff_ref, out_ref):
    blocks, window, cells = out_ref.shape
    chunk = 64
    for block in range(blocks):
        here = slice(block * cells, (block + 1) * cells)

        def rows(at, _):
            first = pl.multiple_of(at * chunk, chunk)
            row = lax.broadcasted_iota(jnp.int32, (chunk, cells), 0) + first
            total = jnp.zeros((chunk, cells), F32)
            for k in range(index_ref.shape[0]):
                total += jnp.where(index_ref[k : k + 1, here] == row, coeff_ref[k : k + 1, here], 0.0)
            out_ref[block, pl.ds(first, chunk), :] = total.astype(BF16)
            return 0

        lax.fori_loop(0, window // chunk, rows, 0)


def decode_kernel(prev_ref, own_ref, next_ref, weave_ref, maps_ref, send_ref):
    table = jnp.concatenate([prev_ref[...], own_ref[...], next_ref[...]], axis=1)
    blocks, window, cells = weave_ref.shape
    step = own_ref.shape[1] // blocks
    share = send_ref.shape[2]
    for block in range(blocks):
        maps = matmul(table[:, block * step : block * step + window], weave_ref[block]).astype(BF16)
        maps_ref[0, :, block * cells : (block + 1) * cells] = maps
        for part in range(cells // share):
            send_ref[block * (cells // share) + part] = maps[:, part * share : (part + 1) * share]


def score_kernel(members_total, cells_total, maps_ref, truth_ref, weight_ref, grad_ref, loss_ref):
    count = members_total
    fairness = (1.0 - ALPHA) / count
    own_share = 1.0 / count
    pair_share = (1.0 - fairness) / (count * (count - 1))
    rows_total, width = truth_ref.shape
    weight = weight_ref[...] / cells_total
    loss = jnp.zeros((1, width), F32)
    for first in range(0, rows_total, 16):
        rows = slice(first, min(first + 16, rows_total))
        maps = [maps_ref[m, rows, :].astype(F32) for m in range(count)]
        truth = truth_ref[rows, :].astype(F32)
        skill = None
        grads = []
        for m in range(count):
            gap = maps[m] - truth
            square = gap * gap + SOFTNESS
            inverse = lax.rsqrt(square)
            size = square * inverse
            skill = size if skill is None else skill + size
            grads.append(gap * inverse * own_share)
        spread = None
        slopes = [None] * count
        for m in range(count):
            for other in range(m + 1, count):
                gap = maps[m] - maps[other]
                square = gap * gap + SOFTNESS
                inverse = lax.rsqrt(square)
                size = square * inverse
                spread = size if spread is None else spread + size
                slope = gap * inverse
                slopes[m] = slope if slopes[m] is None else slopes[m] + slope
                slopes[other] = -slope if slopes[other] is None else slopes[other] - slope
        for m in range(count):
            grad_ref[m, rows, :] = ((grads[m] - pair_share * slopes[m]) * weight).astype(BF16)
        spread_total = 2.0 * spread + count * SOFTNESS**0.5
        score = skill * own_share - (0.5 * pair_share) * spread_total
        loss += jnp.sum(score, axis=0, keepdims=True)
    loss_ref[...] = loss * weight


def gradient_kernel(
    grad_ref,
    loss_ref,
    weave_hbm,
    prev_hbm,
    own_hbm,
    next_hbm,
    out_ref,
    node_grad,
    weave_ref,
    latent_ref,
    arrived,
):
    blocks, window, cells = weave_ref.shape
    copies = [
        pltpu.make_async_copy(weave_hbm.at[block], weave_ref.at[block], arrived.at[block])
        for block in range(blocks)
    ]
    copies += [
        pltpu.make_async_copy(source, latent_ref.at[at], arrived.at[blocks + at])
        for at, source in enumerate((prev_hbm, own_hbm, next_hbm))
    ]
    for copy in copies:
        copy.start()
    nodes = latent_ref.shape[1]
    step = nodes // blocks
    share = grad_ref.shape[2]
    node_grad[...] = jnp.zeros_like(node_grad)
    for block in range(blocks):
        parts = range(block * cells // share, (block + 1) * cells // share)
        grad = jnp.concatenate([grad_ref[part] for part in parts], axis=1)
        copies[block].wait()
        node_grad[:, block * step : block * step + window] += rows_by_rows(grad, weave_ref[block])
    terms = node_grad[...].astype(BF16)
    total = jnp.zeros((terms.shape[0], latent_ref.shape[2]), F32)
    for at in range(3):
        copies[blocks + at].wait()
        total += matmul(terms[:, at * nodes : (at + 1) * nodes], latent_ref[at])
    rows = total.shape[0]
    loss = jnp.sum(loss_ref[...], axis=1, keepdims=True)
    coarse = loss.astype(BF16).astype(F32)
    pieces, _, lanes = out_ref.shape
    splits = pieces * lanes // total.shape[1]
    each = rows // splits
    spare = out_ref.shape[1] - each
    row = lax.broadcasted_iota(jnp.int32, (spare, lanes), 0)
    tail = jnp.where(row == 0, coarse, jnp.where(row == 1, loss - coarse, 0.0)).astype(BF16)
    for piece in range(pieces):
        first = piece % splits * each
        at = piece // splits * lanes
        part = total[first : first + each, at : at + lanes].astype(BF16)
        out_ref[piece] = jnp.concatenate([part, tail], axis=0)


def join_kernel(lines, each, pieces_ref, gradient_ref, loss_ref):
    pieces, _, lanes = pieces_ref.shape
    for chunk in range(pieces // lines):
        parts = [pieces_ref[chunk * lines + line].astype(F32)[:each] for line in range(lines)]
        gradient_ref[:, chunk * lanes : (chunk + 1) * lanes] = jnp.concatenate(parts, axis=0)
    loss = pieces_ref[0].astype(F32)
    loss_ref[...] = loss[each : each + 1] + loss[each + 1 : each + 2]


def summed_over(value, axes):
    parts = lax.all_to_all(value, axes, split_axis=0, concat_axis=0, tiled=True)
    return jnp.sum(parts.astype(F32), axis=0)


def gathered_over(value, axes):
    copies = jnp.broadcast_to(value[None], (lax.axis_size(axes),) + value.shape)
    return lax.all_to_all(copies, axes, split_axis=0, concat_axis=0, tiled=True)


def on_device(
    vertex_embedding_matrix,
    norm_gain,
    qkv_weight,
    out_weight,
    window_reach,
    decode_weight,
    cell_nodes,
    cell_coeffs,
    targets,
    area_weight,
):
    state = vertex_embedding_matrix[0]
    nodes, width = state.shape
    variables, cells = targets.shape
    seq_count = lax.axis_size(SEQ)
    members = lax.axis_size(MEMBER)
    segment = lax.axis_index(SEQ)
    total_cells = cells * seq_count
    share = cells // members
    onward = [(i, (i + 1) % seq_count) for i in range(seq_count)]
    back = [((i + 1) % seq_count, i) for i in range(seq_count)]

    prev_state = lax.ppermute(state, SEQ, onward)
    next_state = lax.ppermute(state, SEQ, back)

    gain = norm_gain[None, :]
    reach = window_reach[:, None]
    smem = pl.BlockSpec(memory_space=pltpu.SMEM)
    anywhere = pl.BlockSpec(memory_space=pl.ANY)
    vmem = pl.BlockSpec(memory_space=pltpu.VMEM)
    sum_type = jax.ShapeDtypeStruct((nodes, width), F32)
    query, own_acc, own_size, norms, bound = pl.pallas_call(
        own_kernel,
        in_specs=[vmem] * 4,
        out_specs=[vmem] * 5,
        out_shape=[
            jax.ShapeDtypeStruct((nodes, width), BF16),
            sum_type,
            sum_type,
            jax.ShapeDtypeStruct((width // GROUP, PAIR), F32),
            jax.ShapeDtypeStruct((1, PAIR), F32),
        ],
        scratch_shapes=[
            pltpu.VMEM((nodes, width), BF16),
            pltpu.VMEM((nodes, nodes), BF16),
            pltpu.VMEM((width // PAIR, nodes, 2 * PAIR), BF16),
        ],
        compiler_params=params(16),
        cost_estimate=pl.CostEstimate(
            flops=12 * 10**9, bytes_accessed=12 * 10**6, transcendentals=4 * 10**6
        ),
        name="own_window",
    )(state, gain, reach, qkv_weight)

    blocks = BLOCKS
    block = cells // blocks
    block_nodes = nodes // blocks
    window = 2 * nodes + block_nodes
    first = (segment - 1) * nodes + jnp.arange(cells, dtype=jnp.int32) // block * block_nodes
    weave = pl.pallas_call(
        weave_kernel,
        in_specs=[vmem, vmem],
        out_specs=vmem,
        out_shape=jax.ShapeDtypeStruct((blocks, window, block), BF16),
        compiler_params=params(4),
        cost_estimate=pl.CostEstimate(flops=10**9, bytes_accessed=10 * 10**6, transcendentals=0),
        name="weave",
    )(cell_nodes - first[None, :], cell_coeffs)
    query, weave = lax.optimization_barrier((query, weave))

    place = jnp.stack([segment, jnp.int32(seq_count)])
    latent, values = pl.pallas_call(
        halo_kernel,
        in_specs=[smem] + [vmem] * 13,
        out_specs=[vmem, vmem],
        out_shape=[
            jax.ShapeDtypeStruct((nodes, width), BF16),
            jax.ShapeDtypeStruct((variables, nodes), BF16),
        ],
        scratch_shapes=[
            pltpu.VMEM((2 * nodes, width), BF16),
            pltpu.VMEM((2, nodes // 2, 3 * nodes // 2), BF16),
            pltpu.VMEM((width // PAIR, 2 * nodes, 2 * PAIR), BF16),
            pltpu.VMEM((nodes, width), BF16),
        ],
        compiler_params=params(24),
        cost_estimate=pl.CostEstimate(
            flops=20 * 10**9, bytes_accessed=16 * 10**6, transcendentals=6 * 10**6
        ),
        name="halo_window",
    )(
        place,
        prev_state,
        next_state,
        state,
        gain,
        reach,
        query,
        own_acc,
        own_size,
        norms,
        bound,
        qkv_weight,
        out_weight,
        decode_weight.T,
    )

    prev_values = lax.ppermute(values, SEQ, onward)
    next_values = lax.ppermute(values, SEQ, back)
    later_latent, prev_values, next_values = lax.optimization_barrier(
        (latent, prev_values, next_values)
    )
    prev_latent = lax.ppermute(later_latent, SEQ, onward)
    next_latent = lax.ppermute(later_latent, SEQ, back)

    predicted_maps, outgoing = pl.pallas_call(
        decode_kernel,
        in_specs=[vmem] * 4,
        out_specs=[vmem, vmem],
        out_shape=[
            jax.ShapeDtypeStruct((1, variables, cells), BF16),
            jax.ShapeDtypeStruct((members, variables, share), BF16),
        ],
        compiler_params=params(16),
        cost_estimate=pl.CostEstimate(
            flops=10**9, bytes_accessed=12 * 10**6, transcendentals=0
        ),
        name="decode_cells",
    )(prev_values, values, next_values, weave)

    incoming = lax.all_to_all(outgoing, MEMBER, split_axis=0, concat_axis=0, tiled=True)
    member_place = lax.axis_index(MEMBER)
    truth = lax.dynamic_slice_in_dim(targets, member_place * share, share, 1)
    weight = lax.dynamic_slice_in_dim(area_weight, member_place * share, share, 0)[None, :]
    lanes = 128
    grads, loss = pl.pallas_call(
        functools.partial(score_kernel, members, total_cells),
        grid=(share // lanes,),
        in_specs=[
            pl.BlockSpec((members, variables, lanes), lambda i: (0, 0, i)),
            pl.BlockSpec((variables, lanes), lambda i: (0, i)),
            pl.BlockSpec((1, lanes), lambda i: (0, i)),
        ],
        out_specs=[
            pl.BlockSpec((members, variables, lanes), lambda i: (0, 0, i)),
            pl.BlockSpec((1, lanes), lambda i: (0, i)),
        ],
        out_shape=[
            jax.ShapeDtypeStruct((members, variables, share), BF16),
            jax.ShapeDtypeStruct((1, share), F32),
        ],
        compiler_params=params(16),
        cost_estimate=pl.CostEstimate(
            flops=10**8, bytes_accessed=2 * 10**6, transcendentals=2 * 10**6
        ),
        name="score",
    )(incoming, truth, weight)

    own_grads = lax.all_to_all(grads, MEMBER, split_axis=0, concat_axis=0, tiled=True)
    lines = lax.axis_size("y")
    pieces = members * lines
    lanes = width // members
    each = variables // lines
    rows = -(-(each + 2) // 16) * 16
    partial_grad = pl.pallas_call(
        gradient_kernel,
        in_specs=[vmem, vmem] + [anywhere] * 4,
        out_specs=vmem,
        out_shape=jax.ShapeDtypeStruct((pieces, rows, lanes), BF16),
        scratch_shapes=[
            pltpu.VMEM((variables, 3 * nodes), F32),
            pltpu.VMEM((blocks, window, block), BF16),
            pltpu.VMEM((3, nodes, width), BF16),
            pltpu.SemaphoreType.DMA((blocks + 3,)),
        ],
        compiler_params=params(58),
        cost_estimate=pl.CostEstimate(
            flops=2 * 10**9, bytes_accessed=14 * 10**6, transcendentals=0
        ),
        name="gradient",
    )(own_grads, loss, weave, prev_latent, latent, next_latent)

    piece = summed_over(partial_grad, MEMBER + ("y",))
    piece = jnp.sum(gathered_over(piece, "z"), axis=0)
    loss = piece[each : each + 1] + piece[each + 1 : each + 2]
    coarse = lax.reduce_precision(loss, 8, 7)
    piece = jnp.concatenate([piece[:each], coarse, loss - coarse], axis=0)
    piece = jnp.pad(piece, ((0, rows - each - 2), (0, 0))).astype(BF16)
    total = gathered_over(piece, MEMBER + ("y",))
    turned, scoring_penalty = pl.pallas_call(
        functools.partial(join_kernel, lines, each),
        in_specs=[vmem],
        out_specs=[vmem, vmem],
        out_shape=[
            jax.ShapeDtypeStruct((variables, width), F32),
            jax.ShapeDtypeStruct((1, lanes), F32),
        ],
        compiler_params=params(8),
        cost_estimate=pl.CostEstimate(flops=10**6, bytes_accessed=10**6, transcendentals=0),
        name="join_gradient",
    )(total)
    scoring_penalty, readout_matrix_derivative = scoring_penalty[0, 0], turned.T
    return (predicted_maps, scoring_penalty, readout_matrix_derivative)


def solution(mesh):
    by_links = jax.sharding.Mesh(mesh.devices.reshape(4, 2, 8, 4), MEMBER + SEQ)
    placed = (
        P(MEMBER, SEQ, None),
        P(),
        P(),
        P(),
        P(SEQ),
        P(),
        P(None, SEQ),
        P(None, SEQ),
        P(None, SEQ),
        P(SEQ),
    )
    return jax.shard_map(
        on_device,
        mesh=by_links,
        in_specs=placed,
        out_specs=(P(MEMBER, None, SEQ), P(), P()),
        check_vma=False,
    )
```

```python
import functools

import jax
import jax.numpy as jnp
from jax import lax
from jax.experimental import pallas as pl
from jax.experimental.pallas import tpu as pltpu
from jax.sharding import PartitionSpec as P

HEADS = 16
HALF = 512
ALPHA = 0.95
SOFTNESS = 0.01
MASKED = -1e30
LOG2E = 1.4426950408889634
GROUP = 256
BLOCKS = 4
PAIR = 128
SCALE = LOG2E * 64**-0.5
BOUND = (90.0 / SCALE) ** 2
MEMBER = ("x", "core")
SEQ = ("z", "y")
F32 = jnp.float32
BF16 = jnp.bfloat16


def params(mib):
    return pltpu.CompilerParams(vmem_limit_bytes=mib * 1024 * 1024)


def rows_by_rows(left, right):
    return lax.dot_general(left, right, (((1,), (1,)), ((), ())), preferred_element_type=F32)


def matmul(left, right):
    return jnp.dot(left, right, preferred_element_type=F32)


def layer_norm(state, gain):
    wide = state.astype(F32)
    size = jnp.mean(wide * wide, axis=-1, keepdims=True)
    return (wide * lax.rsqrt(size + 1e-05) * gain).astype(BF16)


def split_heads(rows):
    lane = lax.broadcasted_iota(jnp.int32, (rows.shape[0], PAIR), 1)
    first = lane < PAIR // 2
    blank = jnp.zeros((rows.shape[0], PAIR), rows.dtype)
    heads = []
    for at in range(0, rows.shape[1], PAIR):
        pair = rows[:, at : at + PAIR]
        heads.append(jnp.where(first, pair, blank))
        heads.append(jnp.where(first, blank, pair))
    return heads


def head_norms(rows):
    lane, column = grid_of((rows.shape[1], PAIR))
    pick = jnp.where(lane // 64 == column, 1.0, 0.0).astype(BF16)
    wide = rows.astype(F32)
    sizes = matmul((wide * wide).astype(BF16), pick)
    return jnp.max(sizes.reshape(rows.shape[0] // 8, 8, PAIR), axis=0).max(axis=0, keepdims=True)


def side_by_side(left, right):
    lane = lax.broadcasted_iota(jnp.int32, left.shape, 1)
    return jnp.where(lane < PAIR // 2, left, right)


def attend_pair(queries, key, value, mask):
    mixed = []
    for query in queries:
        probs = jnp.exp2(rows_by_rows(query, key) * SCALE).astype(BF16) * mask
        mixed.append(matmul(probs, value))
    return (
        side_by_side(mixed[0][:, :PAIR], mixed[1][:, :PAIR]),
        side_by_side(mixed[0][:, PAIR:], mixed[1][:, PAIR:]),
    )


def halves(nodes):
    return [slice(0, nodes // 2), slice(nodes // 2, nodes)]


def grid_of(shape):
    return [lax.broadcasted_iota(jnp.int32, shape, dim) for dim in range(2)]


def flag(value):
    return jnp.where(value, 1.0, 0.0)


def own_kernel(
    state_ref,
    gain_ref,
    reach_ref,
    weight_ref,
    query_ref,
    acc_ref,
    size_ref,
    norm_ref,
    bound_ref,
    normed,
    mask,
    values,
):
    nodes, width = state_ref.shape
    normed[...] = layer_norm(state_ref[...], gain_ref[...])
    place, spot = grid_of((nodes, nodes))
    mask[...] = flag(jnp.abs(place - spot) <= reach_ref[...]).astype(BF16)
    values[...] = jnp.ones_like(values)
    bound = jnp.zeros((1, PAIR), F32)
    for step, first in enumerate(range(0, width, GROUP)):
        rows = normed[...]
        query = matmul(rows, weight_ref[:, first : first + GROUP]).astype(BF16)
        query_ref[:, first : first + GROUP] = query
        at = width + first
        key = matmul(rows, weight_ref[:, at : at + GROUP]).astype(BF16)
        at = 2 * width + first
        value = matmul(rows, weight_ref[:, at : at + GROUP]).astype(BF16)
        heads = split_heads(query)
        norm = head_norms(query)
        norm_ref[step : step + 1, :] = norm
        bound = jnp.maximum(bound, norm * head_norms(key))
        for pair in range(GROUP // PAIR):
            lanes = slice(pair * PAIR, (pair + 1) * PAIR)
            out = slice(first + pair * PAIR, first + (pair + 1) * PAIR)
            held = first // PAIR + pair
            values[held, :, :PAIR] = value[:, lanes]
            for part in halves(nodes):
                queries = [head[part] for head in heads[2 * pair : 2 * pair + 2]]
                acc_ref[part, out], size_ref[part, out] = attend_pair(
                    queries, key[:, lanes], values[held], mask[part, :]
                )
    bound_ref[...] = bound


def halo_kernel(
    place_ref,
    prev_any,
    next_any,
    state_ref,
    gain_ref,
    reach_ref,
    query_ref,
    acc_ref,
    size_ref,
    norm_ref,
    bound_ref,
    weight_ref,
    out_weight_ref,
    decode_ref,
    latent_ref,
    values_ref,
    normed,
    mask,
    values,
    attended,
    halo,
    arrived,
):
    nodes, width = state_ref.shape
    half = nodes // 2
    has_prev = place_ref[0] > 0
    has_next = place_ref[0] < place_ref[1] - 1
    copies = [
        pltpu.make_async_copy(source, halo.at[side], arrived.at[side])
        for side, source in enumerate((prev_any, next_any))
    ]
    for copy in copies:
        copy.start()
    values[...] = jnp.ones_like(values)
    for part, here in enumerate(halves(nodes)):
        place, key = [axis + part * half for axis in grid_of((half, 3 * half))]
        before = key < nodes
        gap = jnp.where(before, place + nodes - key, key - place)
        there = (before & has_prev) | (~before & has_next)
        mask[part] = flag((gap <= reach_ref[here, :]) & there).astype(BF16)

    for side, copy in enumerate(copies):
        copy.wait()
        normed[side * nodes : (side + 1) * nodes] = layer_norm(halo[side], gain_ref[...])

    bound = bound_ref[...]
    for step, first in enumerate(range(0, width, GROUP)):
        rows = normed[...]
        at = width + first
        key = matmul(rows, weight_ref[:, at : at + GROUP]).astype(BF16)
        at = 2 * width + first
        value = matmul(rows, weight_ref[:, at : at + GROUP]).astype(BF16)
        heads = split_heads(query_ref[:, first : first + GROUP])
        bound = jnp.maximum(bound, norm_ref[step : step + 1, :] * head_norms(key))
        for pair in range(GROUP // PAIR):
            lanes = slice(pair * PAIR, (pair + 1) * PAIR)
            out = slice(first + pair * PAIR, first + (pair + 1) * PAIR)
            held = first // PAIR + pair
            values[held, :, :PAIR] = value[:, lanes]
            for part, here in enumerate(halves(nodes)):
                near = slice(part * half, (part + 3) * half)
                queries = [head[here] for head in heads[2 * pair : 2 * pair + 2]]
                acc, size = attend_pair(queries, key[near, lanes], values[held, near], mask[part])
                acc += acc_ref[here, out]
                size += size_ref[here, out]
                attended[here, out] = (acc / size).astype(BF16)

    @pl.when(jnp.logical_not(jnp.max(bound) <= BOUND))
    def _():
        def one_pair(pair, _):
            first = pl.multiple_of(pair * PAIR, PAIR)
            out = pl.ds(first, PAIR)
            keys_at, values_at = pl.ds(width + first, PAIR), pl.ds(2 * width + first, PAIR)
            key = matmul(normed[...], weight_ref[:, keys_at]).astype(BF16)
            value = matmul(normed[...], weight_ref[:, values_at]).astype(BF16)
            own_rows = layer_norm(state_ref[...], gain_ref[...])
            own_key = matmul(own_rows, weight_ref[:, keys_at]).astype(BF16)
            own_value = matmul(own_rows, weight_ref[:, values_at]).astype(BF16)
            own_place, own_spot = grid_of((nodes, nodes))
            allowed = jnp.abs(own_place - own_spot) <= reach_ref[...]
            heads = split_heads(query_ref[:, out])
            for part, here in enumerate(halves(nodes)):
                near = slice(part * half, (part + 3) * half)
                both = []
                for head in heads:
                    far = rows_by_rows(head[here], key[near]) * SCALE
                    far = jnp.where(mask[part] > 0, far, MASKED)
                    own = rows_by_rows(head[here], own_key) * SCALE
                    own = jnp.where(allowed[here], own, MASKED)
                    top = jnp.maximum(
                        jnp.max(far, axis=1, keepdims=True), jnp.max(own, axis=1, keepdims=True)
                    )
                    far, own = jnp.exp2(far - top), jnp.exp2(own - top)
                    size = jnp.sum(far, axis=1, keepdims=True)
                    size += jnp.sum(own, axis=1, keepdims=True)
                    mixed = matmul(far.astype(BF16), value[near])
                    mixed += matmul(own.astype(BF16), own_value)
                    both.append(mixed / size)
                attended[here, out] = side_by_side(*both).astype(BF16)
            return 0

        lax.fori_loop(0, width // PAIR, one_pair, 0)

    total = state_ref[...].astype(F32) + matmul(attended[...], out_weight_ref[...])
    latent = total.astype(BF16)
    latent_ref[...] = latent
    values_ref[...] = rows_by_rows(decode_ref[...], latent).astype(BF16)


def weave_kernel(index_ref, coeff_ref, out_ref):
    blocks, window, cells = out_ref.shape
    chunk = 64
    for block in range(blocks):
        here = slice(block * cells, (block + 1) * cells)

        def rows(at, _):
            first = pl.multiple_of(at * chunk, chunk)
            row = lax.broadcasted_iota(jnp.int32, (chunk, cells), 0) + first
            total = jnp.zeros((chunk, cells), F32)
            for k in range(index_ref.shape[0]):
                total += jnp.where(index_ref[k : k + 1, here] == row, coeff_ref[k : k + 1, here], 0.0)
            out_ref[block, pl.ds(first, chunk), :] = total.astype(BF16)
            return 0

        lax.fori_loop(0, window // chunk, rows, 0)


def decode_kernel(prev_ref, own_ref, next_ref, weave_ref, maps_ref, send_ref):
    table = jnp.concatenate([prev_ref[...], own_ref[...], next_ref[...]], axis=1)
    blocks, window, cells = weave_ref.shape
    step = own_ref.shape[1] // blocks
    share = send_ref.shape[2]
    for block in range(blocks):
        maps = matmul(table[:, block * step : block * step + window], weave_ref[block]).astype(BF16)
        maps_ref[0, :, block * cells : (block + 1) * cells] = maps
        for part in range(cells // share):
            send_ref[block * (cells // share) + part] = maps[:, part * share : (part + 1) * share]


def score_kernel(members_total, cells_total, maps_ref, truth_ref, weight_ref, grad_ref, loss_ref):
    count = members_total
    fairness = (1.0 - ALPHA) / count
    own_share = 1.0 / count
    pair_share = (1.0 - fairness) / (count * (count - 1))
    rows_total, width = truth_ref.shape
    weight = weight_ref[...] / cells_total
    loss = jnp.zeros((1, width), F32)
    for first in range(0, rows_total, 16):
        rows = slice(first, min(first + 16, rows_total))
        maps = [maps_ref[m, rows, :].astype(F32) for m in range(count)]
        truth = truth_ref[rows, :].astype(F32)
        skill = None
        grads = []
        for m in range(count):
            gap = maps[m] - truth
            square = gap * gap + SOFTNESS
            inverse = lax.rsqrt(square)
            size = square * inverse
            skill = size if skill is None else skill + size
            grads.append(gap * inverse * own_share)
        spread = None
        slopes = [None] * count
        for m in range(count):
            for other in range(m + 1, count):
                gap = maps[m] - maps[other]
                square = gap * gap + SOFTNESS
                inverse = lax.rsqrt(square)
                size = square * inverse
                spread = size if spread is None else spread + size
                slope = gap * inverse
                slopes[m] = slope if slopes[m] is None else slopes[m] + slope
                slopes[other] = -slope if slopes[other] is None else slopes[other] - slope
        for m in range(count):
            grad_ref[m, rows, :] = ((grads[m] - pair_share * slopes[m]) * weight).astype(BF16)
        spread_total = 2.0 * spread + count * SOFTNESS**0.5
        score = skill * own_share - (0.5 * pair_share) * spread_total
        loss += jnp.sum(score, axis=0, keepdims=True)
    loss_ref[...] = loss * weight


def gradient_kernel(
    grad_ref,
    loss_ref,
    weave_hbm,
    prev_hbm,
    own_hbm,
    next_hbm,
    out_ref,
    node_grad,
    weave_ref,
    latent_ref,
    arrived,
):
    blocks, window, cells = weave_ref.shape
    copies = [
        pltpu.make_async_copy(weave_hbm.at[block], weave_ref.at[block], arrived.at[block])
        for block in range(blocks)
    ]
    copies += [
        pltpu.make_async_copy(source, latent_ref.at[at], arrived.at[blocks + at])
        for at, source in enumerate((prev_hbm, own_hbm, next_hbm))
    ]
    for copy in copies:
        copy.start()
    nodes = latent_ref.shape[1]
    step = nodes // blocks
    share = grad_ref.shape[2]
    node_grad[...] = jnp.zeros_like(node_grad)
    for block in range(blocks):
        parts = range(block * cells // share, (block + 1) * cells // share)
        grad = jnp.concatenate([grad_ref[part] for part in parts], axis=1)
        copies[block].wait()
        node_grad[:, block * step : block * step + window] += rows_by_rows(grad, weave_ref[block])
    terms = node_grad[...].astype(BF16)
    total = jnp.zeros((terms.shape[0], latent_ref.shape[2]), F32)
    for at in range(3):
        copies[blocks + at].wait()
        total += matmul(terms[:, at * nodes : (at + 1) * nodes], latent_ref[at])
    rows = total.shape[0]
    loss = jnp.sum(loss_ref[...], axis=1, keepdims=True)
    coarse = loss.astype(BF16).astype(F32)
    pieces, _, lanes = out_ref.shape
    splits = pieces * lanes // total.shape[1]
    each = rows // splits
    spare = out_ref.shape[1] - each
    row = lax.broadcasted_iota(jnp.int32, (spare, lanes), 0)
    tail = jnp.where(row == 0, coarse, jnp.where(row == 1, loss - coarse, 0.0)).astype(BF16)
    for piece in range(pieces):
        first = piece % splits * each
        at = piece // splits * lanes
        part = total[first : first + each, at : at + lanes].astype(BF16)
        out_ref[piece] = jnp.concatenate([part, tail], axis=0)


def join_kernel(lines, each, pieces_ref, gradient_ref, loss_ref):
    pieces, _, lanes = pieces_ref.shape
    for chunk in range(pieces // lines):
        parts = [pieces_ref[chunk * lines + line].astype(F32)[:each] for line in range(lines)]
        gradient_ref[:, chunk * lanes : (chunk + 1) * lanes] = jnp.concatenate(parts, axis=0)
    loss = pieces_ref[0].astype(F32)
    loss_ref[...] = loss[each : each + 1] + loss[each + 1 : each + 2]


def summed_over(value, axes):
    parts = lax.all_to_all(value, axes, split_axis=0, concat_axis=0, tiled=True)
    return jnp.sum(parts.astype(F32), axis=0)


def gathered_over(value, axes):
    copies = jnp.broadcast_to(value[None], (lax.axis_size(axes),) + value.shape)
    return lax.all_to_all(copies, axes, split_axis=0, concat_axis=0, tiled=True)


def on_device(
    vertex_embedding_matrix,
    norm_gain,
    qkv_weight,
    out_weight,
    window_reach,
    decode_weight,
    cell_nodes,
    cell_coeffs,
    targets,
    area_weight,
):
    state = vertex_embedding_matrix[0]
    nodes, width = state.shape
    variables, cells = targets.shape
    seq_count = lax.axis_size(SEQ)
    members = lax.axis_size(MEMBER)
    segment = lax.axis_index(SEQ)
    total_cells = cells * seq_count
    share = cells // members
    onward = [(i, (i + 1) % seq_count) for i in range(seq_count)]
    back = [((i + 1) % seq_count, i) for i in range(seq_count)]

    prev_state = lax.ppermute(state, SEQ, onward)
    next_state = lax.ppermute(state, SEQ, back)

    gain = norm_gain[None, :]
    reach = window_reach[:, None]
    smem = pl.BlockSpec(memory_space=pltpu.SMEM)
    anywhere = pl.BlockSpec(memory_space=pl.ANY)
    vmem = pl.BlockSpec(memory_space=pltpu.VMEM)
    sum_type = jax.ShapeDtypeStruct((nodes, width), F32)
    query, own_acc, own_size, norms, bound = pl.pallas_call(
        own_kernel,
        in_specs=[vmem] * 4,
        out_specs=[vmem] * 5,
        out_shape=[
            jax.ShapeDtypeStruct((nodes, width), BF16),
            sum_type,
            sum_type,
            jax.ShapeDtypeStruct((width // GROUP, PAIR), F32),
            jax.ShapeDtypeStruct((1, PAIR), F32),
        ],
        scratch_shapes=[
            pltpu.VMEM((nodes, width), BF16),
            pltpu.VMEM((nodes, nodes), BF16),
            pltpu.VMEM((width // PAIR, nodes, 2 * PAIR), BF16),
        ],
        compiler_params=params(16),
        cost_estimate=pl.CostEstimate(
            flops=12 * 10**9, bytes_accessed=12 * 10**6, transcendentals=4 * 10**6
        ),
        name="own_window",
    )(state, gain, reach, qkv_weight)

    blocks = BLOCKS
    block = cells // blocks
    block_nodes = nodes // blocks
    window = 2 * nodes + block_nodes
    first = (segment - 1) * nodes + jnp.arange(cells, dtype=jnp.int32) // block * block_nodes
    weave = pl.pallas_call(
        weave_kernel,
        in_specs=[vmem, vmem],
        out_specs=vmem,
        out_shape=jax.ShapeDtypeStruct((blocks, window, block), BF16),
        compiler_params=params(4),
        cost_estimate=pl.CostEstimate(flops=10**9, bytes_accessed=10 * 10**6, transcendentals=0),
        name="weave",
    )(cell_nodes - first[None, :], cell_coeffs)
    query, weave = lax.optimization_barrier((query, weave))

    place = jnp.stack([segment, jnp.int32(seq_count)])
    latent, values = pl.pallas_call(
        halo_kernel,
        in_specs=[smem, anywhere, anywhere] + [vmem] * 11,
        out_specs=[vmem, vmem],
        out_shape=[
            jax.ShapeDtypeStruct((nodes, width), BF16),
            jax.ShapeDtypeStruct((variables, nodes), BF16),
        ],
        scratch_shapes=[
            pltpu.VMEM((2 * nodes, width), BF16),
            pltpu.VMEM((2, nodes // 2, 3 * nodes // 2), BF16),
            pltpu.VMEM((width // PAIR, 2 * nodes, 2 * PAIR), BF16),
            pltpu.VMEM((nodes, width), BF16),
            pltpu.VMEM((2, nodes, width), BF16),
            pltpu.SemaphoreType.DMA((2,)),
        ],
        compiler_params=params(24),
        cost_estimate=pl.CostEstimate(
            flops=20 * 10**9, bytes_accessed=16 * 10**6, transcendentals=6 * 10**6
        ),
        name="halo_window",
    )(
        place,
        prev_state,
        next_state,
        state,
        gain,
        reach,
        query,
        own_acc,
        own_size,
        norms,
        bound,
        qkv_weight,
        out_weight,
        decode_weight.T,
    )

    prev_values = lax.ppermute(values, SEQ, onward)
    next_values = lax.ppermute(values, SEQ, back)
    later_latent, prev_values, next_values = lax.optimization_barrier(
        (latent, prev_values, next_values)
    )
    prev_latent = lax.ppermute(later_latent, SEQ, onward)
    next_latent = lax.ppermute(later_latent, SEQ, back)

    predicted_maps, outgoing = pl.pallas_call(
        decode_kernel,
        in_specs=[vmem] * 4,
        out_specs=[vmem, vmem],
        out_shape=[
            jax.ShapeDtypeStruct((1, variables, cells), BF16),
            jax.ShapeDtypeStruct((members, variables, share), BF16),
        ],
        compiler_params=params(16),
        cost_estimate=pl.CostEstimate(
            flops=10**9, bytes_accessed=12 * 10**6, transcendentals=0
        ),
        name="decode_cells",
    )(prev_values, values, next_values, weave)

    incoming = lax.all_to_all(outgoing, MEMBER, split_axis=0, concat_axis=0, tiled=True)
    member_place = lax.axis_index(MEMBER)
    truth = lax.dynamic_slice_in_dim(targets, member_place * share, share, 1)
    weight = lax.dynamic_slice_in_dim(area_weight, member_place * share, share, 0)[None, :]
    lanes = 128
    grads, loss = pl.pallas_call(
        functools.partial(score_kernel, members, total_cells),
        grid=(share // lanes,),
        in_specs=[
            pl.BlockSpec((members, variables, lanes), lambda i: (0, 0, i)),
            pl.BlockSpec((variables, lanes), lambda i: (0, i)),
            pl.BlockSpec((1, lanes), lambda i: (0, i)),
        ],
        out_specs=[
            pl.BlockSpec((members, variables, lanes), lambda i: (0, 0, i)),
            pl.BlockSpec((1, lanes), lambda i: (0, i)),
        ],
        out_shape=[
            jax.ShapeDtypeStruct((members, variables, share), BF16),
            jax.ShapeDtypeStruct((1, share), F32),
        ],
        compiler_params=params(16),
        cost_estimate=pl.CostEstimate(
            flops=10**8, bytes_accessed=2 * 10**6, transcendentals=2 * 10**6
        ),
        name="score",
    )(incoming, truth, weight)

    own_grads = lax.all_to_all(grads, MEMBER, split_axis=0, concat_axis=0, tiled=True)
    lines = lax.axis_size("y")
    pieces = members * lines
    lanes = width // members
    each = variables // lines
    rows = -(-(each + 2) // 16) * 16
    partial_grad = pl.pallas_call(
        gradient_kernel,
        in_specs=[vmem, vmem] + [anywhere] * 4,
        out_specs=vmem,
        out_shape=jax.ShapeDtypeStruct((pieces, rows, lanes), BF16),
        scratch_shapes=[
            pltpu.VMEM((variables, 3 * nodes), F32),
            pltpu.VMEM((blocks, window, block), BF16),
            pltpu.VMEM((3, nodes, width), BF16),
            pltpu.SemaphoreType.DMA((blocks + 3,)),
        ],
        compiler_params=params(58),
        cost_estimate=pl.CostEstimate(
            flops=2 * 10**9, bytes_accessed=14 * 10**6, transcendentals=0
        ),
        name="gradient",
    )(own_grads, loss, weave, prev_latent, latent, next_latent)

    piece = summed_over(partial_grad, MEMBER + ("y",))
    piece = jnp.sum(gathered_over(piece, "z"), axis=0)
    loss = piece[each : each + 1] + piece[each + 1 : each + 2]
    coarse = lax.reduce_precision(loss, 8, 7)
    piece = jnp.concatenate([piece[:each], coarse, loss - coarse], axis=0)
    piece = jnp.pad(piece, ((0, rows - each - 2), (0, 0))).astype(BF16)
    total = gathered_over(piece, MEMBER + ("y",))
    turned, scoring_penalty = pl.pallas_call(
        functools.partial(join_kernel, lines, each),
        in_specs=[vmem],
        out_specs=[vmem, vmem],
        out_shape=[
            jax.ShapeDtypeStruct((variables, width), F32),
            jax.ShapeDtypeStruct((1, lanes), F32),
        ],
        compiler_params=params(8),
        cost_estimate=pl.CostEstimate(flops=10**6, bytes_accessed=10**6, transcendentals=0),
        name="join_gradient",
    )(total)
    scoring_penalty, readout_matrix_derivative = scoring_penalty[0, 0], turned.T
    return (predicted_maps, scoring_penalty, readout_matrix_derivative)


def solution(mesh):
    by_links = jax.sharding.Mesh(mesh.devices.reshape(4, 2, 8, 4), MEMBER + SEQ)
    placed = (
        P(MEMBER, SEQ, None),
        P(),
        P(),
        P(),
        P(SEQ),
        P(),
        P(None, SEQ),
        P(None, SEQ),
        P(None, SEQ),
        P(SEQ),
    )
    return jax.shard_map(
        on_device,
        mesh=by_links,
        in_specs=placed,
        out_specs=(P(MEMBER, None, SEQ), P(), P()),
        check_vma=False,
    )
```
